512 devices in a mesh: gx: 8 (over y), gy: 16 (over z, core), gz: 4 (over x).
Axes of the slice: x: 4, y: 8, z: 8, core: 2. Of those that a mesh axis runs over, the one named last changes fastest.
Arguments:
- source: float32 [2, 64, 256, 1024], P(None, 'gz', 'gy', 'gx'), may hold values from -6 to 6
- adjoint_guess: float32 [2, 64, 256, 1024], P(None, 'gz', 'gy', 'gx'), may hold values from -6 to 6
- forward_field: float32 [2, 64, 256, 1024], P(None, 'gz', 'gy', 'gx'), may hold values from -6 to 6
- labels: int32 [64, 256, 1024], P('gz', 'gy', 'gx'), may hold values from 0 to 7
- perm_real: float32 [8], replicated, may hold values from 1 to 4
- perm_imag: float32 [8], replicated, may hold values from 0 to 1
Outputs:
- adjoint: float32 [2, 64, 256, 1024], P(None, 'gz', 'gy', 'gx')
- material_grad: float32 [2, 8], replicated
- norms: float32 [3], replicated
The draws below stay inside these ranges and needn't reach their ends.
All inputs are finite; a program needn't handle non-finite values.
Results may differ from the reference program's by a relative error of at most 0.0001.
Values sent between devices are 32-bit elements; how exact they have to be, the bound alone decides.
A program may use at most 64 MiB of HBM per device.

```python
import jax
import jax.numpy as jnp
from jax import lax

NMAT = 8
SWEEPS = 3
CSWEEPS = 2
NX = 1024
NY = 256
NZ = 64


def touch_ends(drawn, rng, smallest, high):
    spot = [jax.random.randint(jax.random.fold_in(rng, axis), (), 0, length) for axis, length in enumerate(drawn.shape)]
    widest = drawn.shape.index(max(drawn.shape))
    next_to = spot[:widest] + [(spot[widest] + 1) % drawn.shape[widest]] + spot[widest + 1:]
    return drawn.at[tuple(spot)].set(smallest).at[tuple(next_to)].set(high)


def levels(rng, shape, shards, least, top_value):
    def one(dim, parts):
        heights = jax.random.uniform(jax.random.fold_in(jax.random.fold_in(rng, 6), dim), (parts,), jnp.float32, least / len(shards), top_value / len(shards))
        return jnp.repeat(jnp.exp(heights), shape[dim] // parts).reshape((-1,) + (1,) * (len(shape) - dim - 1))

    factor_of = one(*shards[0])
    for cut in shards[1:]:
        factor_of = factor_of * one(*cut)
    return factor_of


def gaussian(own_key, dims, deviation, reach, shards=(), held_as=jnp.bfloat16):
    drawn = jax.random.normal(own_key, dims, jnp.float32) * deviation
    if len(shards) > 0:
        drawn = levels(own_key, dims, shards, -0.22, 0.18) * drawn
    return jnp.clip(drawn, min=-reach, max=reach).astype(held_as)


def setup_inputs(seed: int = 0) -> dict:
    keys = jax.random.split(jax.random.key(seed), 7)
    source = gaussian(keys[0], (2, NZ, NY, NX), 1.0, 6.0, ((1, 4), (2, 16), (3, 8)), jnp.float32)
    adjoint_guess = gaussian(keys[1], (2, NZ, NY, NX), 1.0, 6.0, ((1, 4), (2, 16), (3, 8)), jnp.float32)
    forward_field = gaussian(keys[2], (2, NZ, NY, NX), 1.0, 6.0, ((1, 4), (2, 16), (3, 8)), jnp.float32)
    labels = touch_ends(jax.random.randint(keys[3], (NZ, NY, NX), 0, NMAT), jax.random.fold_in(keys[3], 1), 0, NMAT - 1).astype(jnp.int32)
    perm_real = jnp.clip(jax.random.uniform(keys[4], (NMAT,), jnp.float32, 1.0, 4.0), 1.0, 4.0)
    perm_imag = jnp.clip(jax.random.uniform(keys[5], (NMAT,), jnp.float32, 0.0, 1.0), 0.0, 1.0)
    return {"source": source, "adjoint_guess": adjoint_guess, "forward_field": forward_field, "labels": labels, "perm_real": perm_real, "perm_imag": perm_imag}


KH2 = 0.5
SHIFT = 0.5
DAMP = 0.5

def cmul(left, right):
    return jnp.stack([left[0] * right[0] - left[1] * right[1], left[0] * right[1] + left[1] * right[0]])

def neighbours(padded):
    total = padded[:, 2:, 1:-1, 1:-1] + padded[:, :-2, 1:-1, 1:-1]
    total = total + padded[:, 1:-1, 2:, 1:-1] + padded[:, 1:-1, :-2, 1:-1]
    return total + padded[:, 1:-1, 1:-1, 2:] + padded[:, 1:-1, 1:-1, :-2]

def pad_field(field):
    return jnp.pad(field, ((0, 0), (1, 1), (1, 1), (1, 1)))

def coefficients(labels, perm_real, perm_imag):
    eps_re = jnp.zeros(labels.shape, jnp.float32)
    eps_im = jnp.zeros(labels.shape, jnp.float32)
    for material in range(perm_real.shape[0]):
        chosen = labels == material
        eps_re = eps_re + jnp.where(chosen, perm_real[material], 0.0)
        eps_im = eps_im + jnp.where(chosen, perm_imag[material], 0.0)
    shift_re = KH2 * (eps_re + SHIFT * eps_im)
    shift_im = KH2 * (SHIFT * eps_re - eps_im)
    diag_re = 6.0 - shift_re
    diag_im = -shift_im
    denom = diag_re * diag_re + diag_im * diag_im
    shifts = jnp.stack([shift_re, shift_im])
    inverse = jnp.stack([diag_re / denom, -diag_im / denom])
    return (shifts, inverse, eps_re)

def fine_apply(field, padded, shifts):
    return 6.0 * field - neighbours(padded) - cmul(shifts, field)

def coarse_apply(field, padded, coarse_q):
    near = neighbours(padded)
    real_part = 6.0 * field[0] - near[0] - 4.0 * coarse_q * field[1]
    imag_part = 6.0 * field[1] - near[1] + 4.0 * coarse_q * field[0]
    return jnp.stack([real_part, imag_part])

def restrict(field):
    lead = field.shape[:-3]
    zlen, ylen, xlen = field.shape[-3:]
    blocks = field.reshape(lead + (zlen // 2, 2, ylen // 2, 2, xlen // 2, 2))
    return lax.optimization_barrier(jnp.mean(blocks, axis=(-5, -3, -1)))

def prolong(field):
    field = jnp.repeat(field, 2, axis=-1)
    field = jnp.repeat(field, 2, axis=-2)
    return jnp.repeat(field, 2, axis=-3)

def coarse_inverse(coarse_q):
    denom = 36.0 + 16.0 * coarse_q * coarse_q
    return jnp.stack([6.0 / denom, -4.0 * coarse_q / denom])

def reference(source, adjoint_guess, forward_field, labels, perm_real, perm_imag):
    shifts, inverse, eps_re = coefficients(labels, perm_real, perm_imag)
    field = adjoint_guess
    for sweep in range(SWEEPS):
        resid = source - fine_apply(field, pad_field(field), shifts)
        field = field + DAMP * cmul(inverse, resid)
    r_pre = source - fine_apply(field, pad_field(field), shifts)
    rhs = 4.0 * restrict(r_pre)
    coarse_q = restrict(KH2 * eps_re)
    inv_c = coarse_inverse(coarse_q)
    coarse = DAMP * cmul(inv_c, rhs)
    for sweep in range(CSWEEPS - 1):
        coarse = coarse + DAMP * cmul(inv_c, rhs - coarse_apply(coarse, pad_field(coarse), coarse_q))
    adjoint = field + prolong(coarse)
    r_fin = source - fine_apply(adjoint, pad_field(adjoint), shifts)
    cells = float(NX * NY * NZ)
    norms = jnp.sqrt(jnp.stack([jnp.sum(source * source), jnp.sum(r_pre * r_pre), jnp.sum(r_fin * r_fin)]) / cells)
    product = cmul(forward_field, adjoint)
    sums = []
    for material in range(NMAT):
        chosen = labels == material
        sums.append(jnp.stack([jnp.sum(jnp.where(chosen, product[0], 0.0)), jnp.sum(jnp.where(chosen, product[1], 0.0))]))
    material_grad = -KH2 / jnp.sqrt(cells) * jnp.stack(sums, axis=1)
    return (adjoint, material_grad, norms)
```

```python
import functools

import jax
import jax.numpy as jnp
from jax import lax
from jax.experimental import pallas as pl
from jax.experimental.pallas import tpu as pltpu
from jax.sharding import PartitionSpec as P

MESH = pl.DeviceIdType.MESH
NMAT = 8
KH2 = 0.5
SHIFT = 0.5
F32 = jnp.float32
AXES = ("gx", "gy", "gz")


def near_offsets():
    return [
        (dx, dy, dz)
        for dx in (-1, 0, 1)
        for dy in (-1, 0, 1)
        for dz in (-1, 0, 1)
        if (dx, dy, dz) != (0, 0, 0)
    ]


def kernel(
    sizes,
    guess_hbm,
    source_hbm,
    forward_hbm,
    labels_hbm,
    pr_ref,
    pi_ref,
    adj_hbm,
    row_ref,
    F,
    B,
    H,
    D,
    FW,
    LI,
    RP,
    E,
    E1,
    G,
    ADJ,
    ER,
    TB,
    PU,
    PL,
    PG,
    PE,
    RU,
    RL,
    RG,
    RE,
    ACC,
    VAL,
    R1,
    R2,
    local_sem,
    send_a,
    recv_a,
    send_c,
    recv_c,
    send_r,
    recv_r,
):
    nx, ny, nz = sizes
    gx, gy, gz = (lax.axis_index(a) for a in AXES)

    def device(offset):
        dx, dy, dz = offset
        return {
            "gx": lax.rem(gx + (dx % nx), nx),
            "gy": lax.rem(gy + (dy % ny), ny),
            "gz": lax.rem(gz + (dz % nz), nz),
        }

    loads = [
        pltpu.make_async_copy(labels_hbm, LI, local_sem.at[0]),
        pltpu.make_async_copy(guess_hbm, F.at[0:2, 0, pl.ds(4, 16), pl.ds(8, 16)], local_sem.at[1]),
        pltpu.make_async_copy(source_hbm, F.at[2:4, 0, pl.ds(4, 16), pl.ds(8, 16)], local_sem.at[2]),
        pltpu.make_async_copy(forward_hbm, FW, local_sem.at[3]),
    ]
    for copy in loads:
        copy.start()

    y_peers = [(0, dy, 0) for dy in range(1, ny)]
    xz_peers = [(dx, 0, dz) for dx in range(nx) for dz in range(nz) if (dx, dz) != (0, 0)]
    met = {(dx % nx, dy % ny, dz % nz) for dx, dy, dz in near_offsets() + y_peers + xz_peers}
    barrier = pltpu.get_barrier_semaphore()
    for offset in sorted(met):
        pl.semaphore_signal(barrier, inc=1, device_id=device(offset), device_id_type=MESH)

    lane = lax.broadcasted_iota(jnp.int32, (8, 128), 1)
    row8 = lax.broadcasted_iota(jnp.int32, (8, 128), 0)
    even_lane = lane % 2 == 0
    even_row = row8 % 2 == 0
    left_half = lane % 8 < 4
    slot_of = lane // 8
    left_ok = (gx > 0).astype(F32)
    right_ok = (gx < nx - 1).astype(F32)
    side_ok = jnp.where(lane < 64, right_ok, left_ok)
    slot_ok = jnp.where(left_half, left_ok, right_ok)

    for m in range(NMAT):
        er = jnp.full((8, 128), pr_ref[m], F32)
        ei = jnp.full((8, 128), pi_ref[m], F32)
        dr = 6.0 - KH2 * (er + SHIFT * ei)
        di = -KH2 * (SHIFT * er - ei)
        half = 0.5 / (dr * dr + di * di)
        TB[0, m] = dr * half
        TB[1, m] = -di * half
        TB[2, m] = dr
        TB[3, m] = di
        TB[4, m] = er

    def look_up(label, tables):
        high = label >= 3.5
        rest = jnp.where(high, label - 4.0, label)
        middle = rest >= 1.5
        odd = jnp.where(middle, rest - 2.0, rest) >= 0.5
        out = []
        for t in tables:
            pairs = [jnp.where(odd, TB[t, 2 * i + 1], TB[t, 2 * i]) for i in range(4)]
            quads = [jnp.where(middle, pairs[2 * i + 1], pairs[2 * i]) for i in range(2)]
            out.append(jnp.where(high, quads[1], quads[0]))
        return out

    def block_sum(v):
        v = v + jnp.where(even_row, pltpu.roll(v, 7, 0), pltpu.roll(v, 1, 0))
        return v + jnp.where(even_lane, pltpu.roll(v, 127, 1), pltpu.roll(v, 1, 1))

    loads[0].wait()

    def own_coefficients(z, carry):
        for yh in range(2):
            label = LI[z, 8 * yh : 8 * yh + 8].astype(F32)
            F[4, 0, z + 4, 8 + 8 * yh : 16 + 8 * yh] = label
            hr, hi, dr, di, er = look_up(label, (0, 1, 2, 3, 4))
            H[0, 0, z + 4, 8 + 8 * yh : 16 + 8 * yh] = hr
            H[1, 0, z + 4, 8 + 8 * yh : 16 + 8 * yh] = hi
            D[0, z, 8 * yh : 8 * yh + 8] = dr
            D[1, z, 8 * yh : 8 * yh + 8] = di
            ER[z, 8 * yh : 8 * yh + 8] = er
        return carry

    lax.fori_loop(0, 16, own_coefficients, 0)

    def own_coarse(zc, carry):
        for yh in range(2):
            rows = slice(8 * yh, 8 * yh + 8)
            q4 = (KH2 * 4.0 / 8.0) * block_sum(ER[2 * zc, rows] + ER[2 * zc + 1, rows])
            scale = 0.5 / (36.0 + q4 * q4)
            G[0, 0, zc + 2, 8 + 8 * yh : 16 + 8 * yh] = 6.0 * scale
            G[1, 0, zc + 2, 8 + 8 * yh : 16 + 8 * yh] = -q4 * scale
        return carry

    lax.fori_loop(0, 8, own_coarse, 0)

    def pack(pieces):
        total = jnp.zeros((8, 128), F32)
        for slot, piece in enumerate(pieces):
            total = jnp.where(slot_of == slot, pltpu.roll(piece, (8 * slot + 4) % 128, 1), total)
        return total

    for yh in range(2):
        rows = slice(8 + 8 * yh, 16 + 8 * yh)
        PL[yh] = pack([F[4, 0, 4 + z, rows] for z in range(16)])
        PG[yh] = pack([G[c, 0, 2 + z, rows] for c in range(2) for z in range(8)])
    loads[1].wait()
    loads[2].wait()

    def pack_quarter(zq, carry):
        for yh in range(2):
            rows = slice(8 + 8 * yh, 16 + 8 * yh)
            PU[zq, yh] = pack([F[f, 0, 4 + 4 * zq + p, rows] for f in range(4) for p in range(4)])
        return carry

    lax.fori_loop(0, 4, pack_quarter, 0)

    def planes(dz, own, deep, at):
        if dz == 0:
            return pl.ds(at, own), pl.ds(at, own)
        if dz > 0:
            return pl.ds(at + own - deep, deep), pl.ds(at - deep, deep)
        return pl.ds(at, deep), pl.ds(at + own, deep)

    started = []

    def send(offset, source, target, sends, receives):
        k = len(started)
        copy = pltpu.make_async_remote_copy(
            src_ref=source,
            dst_ref=target,
            send_sem=sends.at[k],
            recv_sem=receives.at[k],
            device_id=device(offset),
            device_id_type=MESH,
        )
        copy.start()
        started.append(copy)

    pl.semaphore_wait(barrier, len(met))

    for offset in near_offsets():
        dx, dy, dz = offset
        if dx == 0:
            from_z, to_z = planes(dz, 16, 4, 4)
            from_y, to_y = planes(dy, 16, 4, 8)
            send(offset, F.at[:, 0, from_z, from_y], F.at[:, 0, to_z, to_y], send_a, recv_a)
        else:
            side = 0 if dx > 0 else 1
            from_z, to_z = planes(dz, 4, 1, 1)
            from_y, to_y = planes(dy, 2, 1, 1)
            from_z = pl.ds(from_z.start - 1, from_z.size)
            from_y = pl.ds(from_y.start - 1, from_y.size)
            send(offset, PU.at[from_z, from_y], RU.at[side, to_z, to_y], send_a, recv_a)
            send(offset, PL.at[from_y], RL.at[side, 1 - dz, to_y], send_a, recv_a)
    for offset in ((0, 0, 1), (0, 0, -1), (0, 1, 0), (0, -1, 0)):
        from_z, to_z = planes(offset[2], 8, 1, 2)
        from_y, to_y = planes(offset[1], 16, 4, 8)
        send(offset, G.at[:, 0, from_z, from_y], G.at[:, 0, to_z, to_y], send_a, recv_a)
    for offset in ((1, 0, 0), (-1, 0, 0)):
        send(offset, PG, RG.at[0 if offset[0] > 0 else 1], send_a, recv_a)

    for copy in started:
        copy.wait()
    loads[3].wait()

    def merged(low, high):
        return jnp.where(left_half, low, high) * slot_ok

    def unpack_quarter(zq, carry):
        for yg in range(4):
            both = merged(RU[0, zq, yg], RU[1, zq, yg])
            for f in range(4):
                for p in range(4):
                    slot = 4 * f + p
                    F[f, 1, 4 * zq + p, 8 * yg : 8 * yg + 8] = pltpu.roll(both, (124 - 8 * slot) % 128, 1)
        return carry

    lax.fori_loop(0, 6, unpack_quarter, 0)

    y_ok = [(gy > 0).astype(F32), 1.0, 1.0, (gy < ny - 1).astype(F32)]

    def halo_coefficients(z, carry):
        z_ok = ((z >= 4) | (gz > 0)).astype(F32) * ((z < 20) | (gz < nz - 1)).astype(F32)
        part = (z + 12) // 16
        shift = 124 - 8 * lax.rem(z + 12, 16)
        for yg in range(4):
            rows = slice(8 * yg, 8 * yg + 8)
            label = pltpu.roll(merged(RL[0, part, yg], RL[1, part, yg]), shift, 1)
            hr, hi = look_up(label, (0, 1))
            ok = side_ok * (z_ok * y_ok[yg])
            H[0, 1, z, rows] = hr * ok
            H[1, 1, z, rows] = hi * ok
        for yg in (0, 3):
            rows = slice(8 * yg, 8 * yg + 8)
            hr, hi = look_up(F[4, 0, z, rows], (0, 1))
            ok = z_ok * y_ok[yg]
            H[0, 0, z, rows] = hr * ok
            H[1, 0, z, rows] = hi * ok
        return carry

    lax.fori_loop(1, 23, halo_coefficients, 0)

    def halo_planes(z, carry):
        low_ok, high_ok = (gz > 0).astype(F32), (gz < nz - 1).astype(F32)
        for at, ok in ((z, low_ok), (z + 19, high_ok)):
            for yg in (1, 2):
                rows = slice(8 * yg, 8 * yg + 8)
                hr, hi = look_up(F[4, 0, at, rows], (0, 1))
                H[0, 0, at, rows] = hr * ok
                H[1, 0, at, rows] = hi * ok
        return carry

    lax.fori_loop(1, 4, halo_planes, 0)

    @pl.when(gz == 0)
    def _():
        F[0:2, :, 0:4] = jnp.zeros((2, 2, 4, 32, 128), F32)
        G[:, 0, 1] = jnp.zeros((2, 32, 128), F32)

    @pl.when(gz == nz - 1)
    def _():
        F[0:2, :, 20:24] = jnp.zeros((2, 2, 4, 32, 128), F32)
        G[:, 0, 10] = jnp.zeros((2, 32, 128), F32)

    @pl.when(gy == 0)
    def _():
        F[0:2, :, :, 0:8] = jnp.zeros((2, 2, 24, 8, 128), F32)
        G[:, 0, :, 0:8] = jnp.zeros((2, 12, 8, 128), F32)

    @pl.when(gy == ny - 1)
    def _():
        F[0:2, :, :, 24:32] = jnp.zeros((2, 2, 24, 8, 128), F32)
        G[:, 0, :, 24:32] = jnp.zeros((2, 12, 8, 128), F32)

    for yh in range(2):
        both = merged(RG[0, yh], RG[1, yh])
        for c in range(2):
            for z in range(8):
                G[c, 1, 2 + z, 8 + 8 * yh : 16 + 8 * yh] = pltpu.roll(both, (124 - 8 * (8 * c + z)) % 128, 1)

    def across(main, ext, step, tiles):
        at = lax.broadcasted_iota(jnp.int32, main.shape, 1)
        low, high = at < step, at >= 128 - step
        ml, el = pltpu.roll(main, step, 1), pltpu.roll(ext, step, 1)
        mr, er = pltpu.roll(main, 128 - step, 1), pltpu.roll(ext, 128 - step, 1)
        out = [jnp.where(low, el, ml) + jnp.where(high, er, mr)]
        if tiles == 2:
            out.append(jnp.where(low, ml, el) + jnp.where(high, mr, er))
        return out

    def sweep(source, target, first, last):
        def plane(z, carry):
            for rows in (4, 12, 20):
                mid = pl.ds(rows, 8)
                near = [[None, None], [None, None]]
                centre = [[None, None], [None, None]]
                for c in range(2):
                    main, ext = source[c, 0, z, mid], source[c, 1, z, mid]
                    centre[c] = [main, ext]
                    side = across(main, ext, 1, 2)
                    for t in range(2):
                        near[c][t] = (
                            side[t]
                            + (source[c, t, z - 1, mid] + source[c, t, z + 1, mid])
                            + (source[c, t, z, pl.ds(rows - 1, 8)] + source[c, t, z, pl.ds(rows + 1, 8)])
                        )
                for t in range(2):
                    wr = F[2, t, z, mid] + near[0][t]
                    wi = F[3, t, z, mid] + near[1][t]
                    hr, hi = H[0, t, z, mid], H[1, t, z, mid]
                    target[0, t, z, mid] = 0.5 * centre[0][t] + (hr * wr - hi * wi)
                    target[1, t, z, mid] = 0.5 * centre[1][t] + (hr * wi + hi * wr)
            return carry

        lax.fori_loop(first, last, plane, 0)

    sweep(F, B, 1, 23)
    sweep(B, F, 2, 22)
    sweep(F, B, 3, 21)

    zero = jnp.zeros((8, 128), F32)

    def residual(zc, carry):
        src_sq, pre_sq = carry
        for yh in range(2):
            rows = 8 + 8 * yh
            mid, out = pl.ds(rows, 8), slice(8 * yh, 8 * yh + 8)
            sums = [zero, zero]
            for k in range(2):
                z = 2 * zc + k
                near, centre = [], []
                for c in range(2):
                    main = B[c, 0, z + 4, mid]
                    centre.append(main)
                    side = across(main, B[c, 1, z + 4, mid], 1, 1)[0]
                    near.append(
                        side
                        + (B[c, 0, z + 3, mid] + B[c, 0, z + 5, mid])
                        + (B[c, 0, z + 4, pl.ds(rows - 1, 8)] + B[c, 0, z + 4, pl.ds(rows + 1, 8)])
                    )
                dr, di = D[0, z, out], D[1, z, out]
                sr, si = F[2, 0, z + 4, mid], F[3, 0, z + 4, mid]
                rr = sr + near[0] - (dr * centre[0] - di * centre[1])
                ri = si + near[1] - (dr * centre[1] + di * centre[0])
                RP[0, z, out] = rr
                RP[1, z, out] = ri
                src_sq = src_sq + (sr * sr + si * si)
                pre_sq = pre_sq + (rr * rr + ri * ri)
                sums = [sums[0] + rr, sums[1] + ri]
            br, bi = 0.5 * block_sum(sums[0]), 0.5 * block_sum(sums[1])
            wr, wi = G[0, 0, zc + 2, mid], G[1, 0, zc + 2, mid]
            E[0, 0, zc + 2, mid] = wr * br - wi * bi
            E[1, 0, zc + 2, mid] = wr * bi + wi * br
        return src_sq, pre_sq

    src_sq, pre_sq = lax.fori_loop(0, 8, residual, (zero, zero))

    for yh in range(2):
        PE[yh] = pack([E[c, 0, 2 + z, 8 + 8 * yh : 16 + 8 * yh] for c in range(2) for z in range(8)])
    del started[:]
    for offset in near_offsets():
        dx, dy, dz = offset
        if dx and dy and dz:
            continue
        if dx == 0:
            from_z, to_z = planes(dz, 8, 1 if dy else 2, 2)
            from_y, to_y = planes(dy, 16, 4, 8)
            send(offset, E.at[:, 0, from_z, from_y], E.at[:, 0, to_z, to_y], send_c, recv_c)
        else:
            side = 0 if dx > 0 else 1
            from_y, to_y = planes(dy, 2, 1, 1)
            from_y = pl.ds(from_y.start - 1, from_y.size)
            send(offset, PE.at[from_y], RE.at[side, 1 - dz, to_y], send_c, recv_c)
    for copy in started:
        copy.wait()

    for part, where in ((1, range(8)), (0, (7,)), (2, (0,))):
        for yg in range(4) if part == 1 else (1, 2):
            both = merged(RE[0, part, yg], RE[1, part, yg])
            for c in range(2):
                for z in where:
                    at = 2 + z if part == 1 else (1 if part == 0 else 10)
                    E[c, 1, at, 8 * yg : 8 * yg + 8] = pltpu.roll(both, (124 - 8 * (8 * c + z)) % 128, 1)

    @pl.when(gz == 0)
    def _():
        E[:, :, 0:2] = jnp.zeros((2, 2, 2, 32, 128), F32)

    @pl.when(gz == nz - 1)
    def _():
        E[:, :, 10:12] = jnp.zeros((2, 2, 2, 32, 128), F32)

    @pl.when(gy == 0)
    def _():
        E[:, :, :, 0:8] = jnp.zeros((2, 2, 12, 8, 128), F32)

    @pl.when(gy == ny - 1)
    def _():
        E[:, :, :, 24:32] = jnp.zeros((2, 2, 12, 8, 128), F32)

    def coarse(zc, row_groups, tiles):
        for rows in row_groups:
            mid = pl.ds(rows, 8)
            near, centre = [], []
            for c in range(2):
                main, ext = E[c, 0, zc, mid], E[c, 1, zc, mid]
                side = across(main, ext, 2, tiles)
                centre.append([main, ext])
                near.append(
                    [
                        side[t]
                        + (E[c, t, zc - 1, mid] + E[c, t, zc + 1, mid])
                        + (E[c, t, zc, pl.ds(rows - 2, 8)] + E[c, t, zc, pl.ds(rows + 2, 8)])
                        for t in range(tiles)
                    ]
                )
            for t in range(tiles):
                wr, wi = G[0, t, zc, mid], G[1, t, zc, mid]
                E1[0, t, zc, mid] = 1.5 * centre[0][t] + (wr * near[0][t] - wi * near[1][t])
                E1[1, t, zc, mid] = 1.5 * centre[1][t] + (wr * near[1][t] + wi * near[0][t])

    def own_planes(zc, carry):
        coarse(zc, (8, 16), 2)
        coarse(zc, (4, 20), 1)
        return carry

    lax.fori_loop(2, 10, own_planes, 0)
    coarse(1, (8, 16), 1)
    coarse(10, (8, 16), 1)

    def correct(zc, carry):
        carry = list(carry)
        for yh in range(2):
            rows = 8 + 8 * yh
            mid, out = pl.ds(rows, 8), slice(8 * yh, 8 * yh + 8)
            e, base = [], []
            for c in range(2):
                main = E1[c, 0, zc + 2, mid]
                side = across(main, E1[c, 1, zc + 2, mid], 1, 1)[0]
                e.append(main)
                base.append(
                    main + side + (E1[c, 0, zc + 2, pl.ds(rows - 1, 8)] + E1[c, 0, zc + 2, pl.ds(rows + 1, 8)])
                )
            for k in range(2):
                z = 2 * zc + k
                dr, di = D[0, z, out], D[1, z, out]
                rr = RP[0, z, out] + (base[0] + E1[0, 0, zc + 1 + 2 * k, mid]) - (dr * e[0] - di * e[1])
                ri = RP[1, z, out] + (base[1] + E1[1, 0, zc + 1 + 2 * k, mid]) - (dr * e[1] + di * e[0])
                carry[0] = carry[0] + (rr * rr + ri * ri)
                ar = B[0, 0, z + 4, mid] + e[0]
                ai = B[1, 0, z + 4, mid] + e[1]
                ADJ[0, z, out] = ar
                ADJ[1, z, out] = ai
                fr, fi = FW[0, z, out], FW[1, z, out]
                pr = fr * ar - fi * ai
                pi = fr * ai + fi * ar
                label = LI[z, out]
                for m in range(NMAT):
                    chosen = label == m
                    carry[1 + m] = carry[1 + m] + jnp.where(chosen, pr, 0.0)
                    carry[9 + m] = carry[9 + m] + jnp.where(chosen, pi, 0.0)
        return tuple(carry)

    sums = lax.fori_loop(0, 8, correct, (zero,) * 17)
    store = pltpu.make_async_copy(ADJ, adj_hbm, local_sem.at[0])
    store.start()

    ordered = list(sums[1:]) + [src_sq, pre_sq, sums[0]]
    ACC[...] = jnp.zeros((24, 128), F32)
    for k, value in enumerate(ordered):
        ACC[k : k + 1] = jnp.sum(value, axis=0, keepdims=True)
    totals = jnp.sum(ACC[...], axis=1, keepdims=True)
    lane24 = lax.broadcasted_iota(jnp.int32, (24, 128), 1)
    row24 = lax.broadcasted_iota(jnp.int32, (24, 128), 0)
    row = jnp.sum(jnp.where(lane24 == row24, totals, 0.0), axis=0, keepdims=True)

    for stage, (peers, slots, own) in enumerate(((y_peers, R1, gy), (xz_peers, R2, gx * nz + gz))):
        count = len(peers)
        VAL[stage] = row
        for offset in peers:
            pltpu.make_async_remote_copy(
                src_ref=VAL.at[stage],
                dst_ref=slots.at[own],
                send_sem=send_r.at[stage],
                recv_sem=recv_r.at[stage],
                device_id=device(offset),
                device_id_type=MESH,
            ).start()
        slots[own] = row
        every = pltpu.make_async_remote_copy(
            src_ref=slots.at[pl.ds(0, count)],
            dst_ref=slots.at[pl.ds(0, count)],
            send_sem=send_r.at[stage],
            recv_sem=recv_r.at[stage],
            device_id=device(peers[0]),
            device_id_type=MESH,
        )
        every.wait_recv()
        every.wait_send()
        row = slots[0]
        for k in range(1, count + 1):
            row = row + slots[k]

    cells = float(nx * ny * nz * 16 * 16 * 128)
    one = lax.broadcasted_iota(jnp.int32, (1, 128), 1)
    row_ref[...] = jnp.where(one < 2 * NMAT, (-KH2 / cells**0.5) * row, jnp.sqrt(jnp.maximum(row, 0.0) / cells))
    store.wait()


def shards(sizes, source, adjoint_guess, forward_field, labels, perm_real, perm_imag):
    vmem = lambda *shape: pltpu.VMEM(shape, F32)
    dma = pltpu.SemaphoreType.DMA
    n_a, n_c = 50, 18
    adjoint, row = pl.pallas_call(
        functools.partial(kernel, sizes),
        out_shape=(
            jax.ShapeDtypeStruct(adjoint_guess.shape, F32),
            jax.ShapeDtypeStruct((1, 128), F32),
        ),
        in_specs=[pl.BlockSpec(memory_space=pl.ANY)] * 4 + [pl.BlockSpec(memory_space=pltpu.SMEM)] * 2,
        out_specs=(pl.BlockSpec(memory_space=pl.ANY), pl.BlockSpec(memory_space=pltpu.VMEM)),
        scratch_shapes=[
            vmem(5, 2, 24, 32, 128),
            vmem(2, 2, 24, 32, 128),
            vmem(2, 2, 24, 32, 128),
            vmem(2, 16, 16, 128),
            vmem(2, 16, 16, 128),
            pltpu.VMEM((16, 16, 128), jnp.int32),
            vmem(2, 16, 16, 128),
            vmem(2, 2, 12, 32, 128),
            vmem(2, 2, 12, 32, 128),
            vmem(2, 2, 12, 32, 128),
            vmem(2, 16, 16, 128),
            vmem(16, 16, 128),
            vmem(5, 8, 8, 128),
            vmem(4, 2, 8, 128),
            vmem(2, 8, 128),
            vmem(2, 8, 128),
            vmem(2, 8, 128),
            vmem(2, 6, 4, 8, 128),
            vmem(2, 3, 4, 8, 128),
            vmem(2, 2, 8, 128),
            vmem(2, 3, 4, 8, 128),
            vmem(24, 128),
            vmem(2, 1, 128),
            vmem(sizes[1], 1, 128),
            vmem(sizes[0] * sizes[2], 1, 128),
            dma((4,)),
            dma((n_a,)),
            dma((n_a,)),
            dma((n_c,)),
            dma((n_c,)),
            dma((2,)),
            dma((2,)),
        ],
        compiler_params=pltpu.CompilerParams(collective_id=0, has_side_effects=True, vmem_limit_bytes=40 << 20),
    )(adjoint_guess, source, forward_field, labels, perm_real, perm_imag)
    material_grad = row[0, : 2 * NMAT].reshape(2, NMAT)
    norms = row[0, 2 * NMAT : 2 * NMAT + 3]
    return adjoint, material_grad, norms


def solution(mesh):
    sizes = tuple(mesh.shape[a] for a in AXES)
    field = P(None, "gz", "gy", "gx")
    return jax.shard_map(
        functools.partial(shards, sizes),
        mesh=mesh,
        in_specs=(field, field, field, P("gz", "gy", "gx"), P(), P()),
        out_specs=(field, P(), P()),
        check_vma=False,
    )
```

```python
import functools

import jax
import jax.numpy as jnp
from jax import lax
from jax.experimental import pallas as pl
from jax.experimental.pallas import tpu as pltpu
from jax.sharding import PartitionSpec as P

MESH = pl.DeviceIdType.MESH
NMAT = 8
KH2 = 0.5
SHIFT = 0.5
F32 = jnp.float32
AXES = ("gx", "gy", "gz")


def near_offsets():
    return [
        (dx, dy, dz)
        for dx in (-1, 0, 1)
        for dy in (-1, 0, 1)
        for dz in (-1, 0, 1)
        if (dx, dy, dz) != (0, 0, 0)
    ]


def kernel(
    sizes,
    guess_hbm,
    source_hbm,
    forward_hbm,
    labels_hbm,
    pr_ref,
    pi_ref,
    adj_hbm,
    row_ref,
    F,
    B,
    H,
    D,
    FW,
    LI,
    RP,
    E,
    E1,
    G,
    ADJ,
    ER,
    TB,
    PU,
    PL,
    PG,
    PE,
    RU,
    RL,
    RG,
    RE,
    ACC,
    VAL,
    R1,
    R2,
    local_sem,
    send_a,
    recv_a,
    send_c,
    recv_c,
    send_r,
    recv_r,
    ready,
):
    nx, ny, nz = sizes
    gx, gy, gz = (lax.axis_index(a) for a in AXES)

    def device(offset):
        dx, dy, dz = offset
        return {
            "gx": lax.rem(gx + (dx % nx), nx),
            "gy": lax.rem(gy + (dy % ny), ny),
            "gz": lax.rem(gz + (dz % nz), nz),
        }

    loads = [
        pltpu.make_async_copy(labels_hbm, LI, local_sem.at[0]),
        pltpu.make_async_copy(guess_hbm, F.at[0:2, 0, pl.ds(4, 16), pl.ds(8, 16)], local_sem.at[1]),
        pltpu.make_async_copy(source_hbm, F.at[2:4, 0, pl.ds(4, 16), pl.ds(8, 16)], local_sem.at[2]),
        pltpu.make_async_copy(forward_hbm, FW, local_sem.at[3]),
    ]
    for copy in loads:
        copy.start()

    y_peers = [(0, dy, 0) for dy in range(1, ny)]
    xz_peers = [(dx, 0, dz) for dx in range(nx) for dz in range(nz) if (dx, dz) != (0, 0)]

    def greet(semaphore, offsets):
        offsets = {(dx % nx, dy % ny, dz % nz) for dx, dy, dz in offsets}
        for offset in sorted(offsets):
            pl.semaphore_signal(semaphore, inc=1, device_id=device(offset), device_id_type=MESH)
        return len(offsets)

    barrier = pltpu.get_barrier_semaphore()
    met = greet(barrier, near_offsets())

    lane = lax.broadcasted_iota(jnp.int32, (8, 128), 1)
    row8 = lax.broadcasted_iota(jnp.int32, (8, 128), 0)
    even_lane = lane % 2 == 0
    even_row = row8 % 2 == 0
    left_half = lane % 8 < 4
    slot_of = lane // 8
    left_ok = (gx > 0).astype(F32)
    right_ok = (gx < nx - 1).astype(F32)
    side_ok = jnp.where(lane < 64, right_ok, left_ok)
    slot_ok = jnp.where(left_half, left_ok, right_ok)

    for m in range(NMAT):
        er = jnp.full((8, 128), pr_ref[m], F32)
        ei = jnp.full((8, 128), pi_ref[m], F32)
        dr = 6.0 - KH2 * (er + SHIFT * ei)
        di = -KH2 * (SHIFT * er - ei)
        half = 0.5 / (dr * dr + di * di)
        TB[0, m] = dr * half
        TB[1, m] = -di * half
        TB[2, m] = dr
        TB[3, m] = di
        TB[4, m] = er

    def look_up(label, tables):
        high = label >= 3.5
        rest = jnp.where(high, label - 4.0, label)
        middle = rest >= 1.5
        odd = jnp.where(middle, rest - 2.0, rest) >= 0.5
        out = []
        for t in tables:
            pairs = [jnp.where(odd, TB[t, 2 * i + 1], TB[t, 2 * i]) for i in range(4)]
            quads = [jnp.where(middle, pairs[2 * i + 1], pairs[2 * i]) for i in range(2)]
            out.append(jnp.where(high, quads[1], quads[0]))
        return out

    def block_sum(v):
        v = v + jnp.where(even_row, pltpu.roll(v, 7, 0), pltpu.roll(v, 1, 0))
        return v + jnp.where(even_lane, pltpu.roll(v, 127, 1), pltpu.roll(v, 1, 1))

    loads[0].wait()

    def own_coefficients(z, carry):
        for yh in range(2):
            label = LI[z, 8 * yh : 8 * yh + 8].astype(F32)
            F[4, 0, z + 4, 8 + 8 * yh : 16 + 8 * yh] = label
            hr, hi, dr, di, er = look_up(label, (0, 1, 2, 3, 4))
            H[0, 0, z + 4, 8 + 8 * yh : 16 + 8 * yh] = hr
            H[1, 0, z + 4, 8 + 8 * yh : 16 + 8 * yh] = hi
            D[0, z, 8 * yh : 8 * yh + 8] = dr
            D[1, z, 8 * yh : 8 * yh + 8] = di
            ER[z, 8 * yh : 8 * yh + 8] = er
        return carry

    lax.fori_loop(0, 16, own_coefficients, 0, unroll=4)

    def own_coarse(zc, carry):
        for yh in range(2):
            rows = slice(8 * yh, 8 * yh + 8)
            q4 = (KH2 * 4.0 / 8.0) * block_sum(ER[2 * zc, rows] + ER[2 * zc + 1, rows])
            scale = 0.5 / (36.0 + q4 * q4)
            G[0, 0, zc + 2, 8 + 8 * yh : 16 + 8 * yh] = 6.0 * scale
            G[1, 0, zc + 2, 8 + 8 * yh : 16 + 8 * yh] = -q4 * scale
        return carry

    lax.fori_loop(0, 8, own_coarse, 0, unroll=4)

    def pack(pieces):
        total = jnp.zeros((8, 128), F32)
        for slot, piece in enumerate(pieces):
            total = jnp.where(slot_of == slot, pltpu.roll(piece, (8 * slot + 4) % 128, 1), total)
        return total

    for yh in range(2):
        rows = slice(8 + 8 * yh, 16 + 8 * yh)
        PL[yh] = pack([F[4, 0, 4 + z, rows] for z in range(16)])
        PG[yh] = pack([G[c, 0, 2 + z, rows] for c in range(2) for z in range(8)])
    loads[1].wait()
    loads[2].wait()

    def pack_quarter(zq, carry):
        for yh in range(2):
            rows = slice(8 + 8 * yh, 16 + 8 * yh)
            PU[zq, yh] = pack([F[f, 0, 4 + 4 * zq + p, rows] for f in range(4) for p in range(4)])
        return carry

    lax.fori_loop(0, 4, pack_quarter, 0, unroll=2)

    def planes(dz, own, deep, at):
        if dz == 0:
            return pl.ds(at, own), pl.ds(at, own)
        if dz > 0:
            return pl.ds(at + own - deep, deep), pl.ds(at - deep, deep)
        return pl.ds(at, deep), pl.ds(at + own, deep)

    started = []

    def send(offset, source, target, sends, receives):
        k = len(started)
        copy = pltpu.make_async_remote_copy(
            src_ref=source,
            dst_ref=target,
            send_sem=sends.at[k],
            recv_sem=receives.at[k],
            device_id=device(offset),
            device_id_type=MESH,
        )
        copy.start()
        started.append(copy)

    pl.semaphore_wait(barrier, met)

    for offset in near_offsets():
        dx, dy, dz = offset
        if dx == 0:
            from_z, to_z = planes(dz, 16, 4, 4)
            from_y, to_y = planes(dy, 16, 4, 8)
            send(offset, F.at[:, 0, from_z, from_y], F.at[:, 0, to_z, to_y], send_a, recv_a)
        else:
            side = 0 if dx > 0 else 1
            from_z, to_z = planes(dz, 4, 1, 1)
            from_y, to_y = planes(dy, 2, 1, 1)
            from_z = pl.ds(from_z.start - 1, from_z.size)
            from_y = pl.ds(from_y.start - 1, from_y.size)
            send(offset, PU.at[from_z, from_y], RU.at[side, to_z, to_y], send_a, recv_a)
            send(offset, PL.at[from_y], RL.at[side, 1 - dz, to_y], send_a, recv_a)
    for offset in ((0, 0, 1), (0, 0, -1), (0, 1, 0), (0, -1, 0)):
        from_z, to_z = planes(offset[2], 8, 1, 2)
        from_y, to_y = planes(offset[1], 16, 4, 8)
        send(offset, G.at[:, 0, from_z, from_y], G.at[:, 0, to_z, to_y], send_a, recv_a)
    for offset in ((1, 0, 0), (-1, 0, 0)):
        send(offset, PG, RG.at[0 if offset[0] > 0 else 1], send_a, recv_a)

    met = greet(ready.at[0], [o for o in near_offsets() if o[1] == 0 or (o[0], o[2]) == (0, 0)])

    for copy in started:
        copy.wait()
    loads[3].wait()
    pl.semaphore_wait(ready.at[0], met)
    met = greet(ready.at[1], [(2, 0, 0), (-2, 0, 0), (0, 2, 0), (0, -2, 0)])

    def merged(low, high):
        return jnp.where(left_half, low, high) * slot_ok

    def unpack_quarter(zq, carry):
        for yg in range(4):
            both = merged(RU[0, zq, yg], RU[1, zq, yg])
            for f in range(4):
                for p in range(4):
                    slot = 4 * f + p
                    F[f, 1, 4 * zq + p, 8 * yg : 8 * yg + 8] = pltpu.roll(both, (124 - 8 * slot) % 128, 1)
        return carry

    lax.fori_loop(0, 6, unpack_quarter, 0, unroll=6)

    y_ok = [(gy > 0).astype(F32), 1.0, 1.0, (gy < ny - 1).astype(F32)]

    def halo_coefficients(z, carry):
        z_ok = ((z >= 4) | (gz > 0)).astype(F32) * ((z < 20) | (gz < nz - 1)).astype(F32)
        part = (z + 12) // 16
        shift = 124 - 8 * lax.rem(z + 12, 16)
        for yg in range(4):
            rows = slice(8 * yg, 8 * yg + 8)
            label = pltpu.roll(merged(RL[0, part, yg], RL[1, part, yg]), shift, 1)
            hr, hi = look_up(label, (0, 1))
            ok = side_ok * (z_ok * y_ok[yg])
            H[0, 1, z, rows] = hr * ok
            H[1, 1, z, rows] = hi * ok
        for yg in (0, 3):
            rows = slice(8 * yg, 8 * yg + 8)
            hr, hi = look_up(F[4, 0, z, rows], (0, 1))
            ok = z_ok * y_ok[yg]
            H[0, 0, z, rows] = hr * ok
            H[1, 0, z, rows] = hi * ok
        return carry

    lax.fori_loop(1, 23, halo_coefficients, 0, unroll=11)

    def halo_planes(z, carry):
        low_ok, high_ok = (gz > 0).astype(F32), (gz < nz - 1).astype(F32)
        for at, ok in ((z, low_ok), (z + 19, high_ok)):
            for yg in (1, 2):
                rows = slice(8 * yg, 8 * yg + 8)
                hr, hi = look_up(F[4, 0, at, rows], (0, 1))
                H[0, 0, at, rows] = hr * ok
                H[1, 0, at, rows] = hi * ok
        return carry

    lax.fori_loop(1, 4, halo_planes, 0, unroll=3)

    @pl.when(gz == 0)
    def _():
        F[0:2, :, 0:4] = jnp.zeros((2, 2, 4, 32, 128), F32)
        G[:, 0, 1] = jnp.zeros((2, 32, 128), F32)

    @pl.when(gz == nz - 1)
    def _():
        F[0:2, :, 20:24] = jnp.zeros((2, 2, 4, 32, 128), F32)
        G[:, 0, 10] = jnp.zeros((2, 32, 128), F32)

    @pl.when(gy == 0)
    def _():
        F[0:2, :, :, 0:8] = jnp.zeros((2, 2, 24, 8, 128), F32)
        G[:, 0, :, 0:8] = jnp.zeros((2, 12, 8, 128), F32)

    @pl.when(gy == ny - 1)
    def _():
        F[0:2, :, :, 24:32] = jnp.zeros((2, 2, 24, 8, 128), F32)
        G[:, 0, :, 24:32] = jnp.zeros((2, 12, 8, 128), F32)

    for yh in range(2):
        both = merged(RG[0, yh], RG[1, yh])
        for c in range(2):
            for z in range(8):
                G[c, 1, 2 + z, 8 + 8 * yh : 16 + 8 * yh] = pltpu.roll(both, (124 - 8 * (8 * c + z)) % 128, 1)

    def across(main, ext, step, tiles):
        at = lax.broadcasted_iota(jnp.int32, main.shape, 1)
        low, high = at < step, at >= 128 - step
        ml, el = pltpu.roll(main, step, 1), pltpu.roll(ext, step, 1)
        mr, er = pltpu.roll(main, 128 - step, 1), pltpu.roll(ext, 128 - step, 1)
        out = [jnp.where(low, el, ml) + jnp.where(high, er, mr)]
        if tiles == 2:
            out.append(jnp.where(low, ml, el) + jnp.where(high, mr, er))
        return out

    def sweep(source, target, first, last):
        def plane(z, carry):
            for rows in (4, 12, 20):
                mid = pl.ds(rows, 8)
                near = [[None, None], [None, None]]
                centre = [[None, None], [None, None]]
                for c in range(2):
                    main, ext = source[c, 0, z, mid], source[c, 1, z, mid]
                    centre[c] = [main, ext]
                    side = across(main, ext, 1, 2)
                    for t in range(2):
                        near[c][t] = (
                            side[t]
                            + (source[c, t, z - 1, mid] + source[c, t, z + 1, mid])
                            + (source[c, t, z, pl.ds(rows - 1, 8)] + source[c, t, z, pl.ds(rows + 1, 8)])
                        )
                for t in range(2):
                    wr = F[2, t, z, mid] + near[0][t]
                    wi = F[3, t, z, mid] + near[1][t]
                    hr, hi = H[0, t, z, mid], H[1, t, z, mid]
                    target[0, t, z, mid] = 0.5 * centre[0][t] + (hr * wr - hi * wi)
                    target[1, t, z, mid] = 0.5 * centre[1][t] + (hr * wi + hi * wr)
            return carry

        lax.fori_loop(first, last, plane, 0, unroll=(last - first) // 2)

    sweep(F, B, 1, 23)
    sweep(B, F, 2, 22)
    sweep(F, B, 3, 21)

    pl.semaphore_wait(ready.at[1], met)
    met = greet(ready.at[2], [(0, 4, 0), (0, -4, 0)])

    zero = jnp.zeros((8, 128), F32)

    def residual(zc, carry):
        src_sq, pre_sq = carry
        for yh in range(2):
            rows = 8 + 8 * yh
            mid, out = pl.ds(rows, 8), slice(8 * yh, 8 * yh + 8)
            sums = [zero, zero]
            for k in range(2):
                z = 2 * zc + k
                near, centre = [], []
                for c in range(2):
                    main = B[c, 0, z + 4, mid]
                    centre.append(main)
                    side = across(main, B[c, 1, z + 4, mid], 1, 1)[0]
                    near.append(
                        side
                        + (B[c, 0, z + 3, mid] + B[c, 0, z + 5, mid])
                        + (B[c, 0, z + 4, pl.ds(rows - 1, 8)] + B[c, 0, z + 4, pl.ds(rows + 1, 8)])
                    )
                dr, di = D[0, z, out], D[1, z, out]
                sr, si = F[2, 0, z + 4, mid], F[3, 0, z + 4, mid]
                rr = sr + near[0] - (dr * centre[0] - di * centre[1])
                ri = si + near[1] - (dr * centre[1] + di * centre[0])
                RP[0, z, out] = rr
                RP[1, z, out] = ri
                src_sq = src_sq + (sr * sr + si * si)
                pre_sq = pre_sq + (rr * rr + ri * ri)
                sums = [sums[0] + rr, sums[1] + ri]
            br, bi = 0.5 * block_sum(sums[0]), 0.5 * block_sum(sums[1])
            wr, wi = G[0, 0, zc + 2, mid], G[1, 0, zc + 2, mid]
            E[0, 0, zc + 2, mid] = wr * br - wi * bi
            E[1, 0, zc + 2, mid] = wr * bi + wi * br
        return src_sq, pre_sq

    src_sq, pre_sq = lax.fori_loop(0, 8, residual, (zero, zero), unroll=4)

    for yh in range(2):
        PE[yh] = pack([E[c, 0, 2 + z, 8 + 8 * yh : 16 + 8 * yh] for c in range(2) for z in range(8)])
    del started[:]
    for offset in near_offsets():
        dx, dy, dz = offset
        if dx and dy and dz:
            continue
        if dx == 0:
            from_z, to_z = planes(dz, 8, 1 if dy else 2, 2)
            from_y, to_y = planes(dy, 16, 4, 8)
            send(offset, E.at[:, 0, from_z, from_y], E.at[:, 0, to_z, to_y], send_c, recv_c)
        else:
            side = 0 if dx > 0 else 1
            from_y, to_y = planes(dy, 2, 1, 1)
            from_y = pl.ds(from_y.start - 1, from_y.size)
            send(offset, PE.at[from_y], RE.at[side, 1 - dz, to_y], send_c, recv_c)
    for copy in started:
        copy.wait()

    for part, where in ((1, range(8)), (0, (7,)), (2, (0,))):
        for yg in range(4) if part == 1 else (1, 2):
            both = merged(RE[0, part, yg], RE[1, part, yg])
            for c in range(2):
                for z in where:
                    at = 2 + z if part == 1 else (1 if part == 0 else 10)
                    E[c, 1, at, 8 * yg : 8 * yg + 8] = pltpu.roll(both, (124 - 8 * (8 * c + z)) % 128, 1)

    @pl.when(gz == 0)
    def _():
        E[:, :, 0:2] = jnp.zeros((2, 2, 2, 32, 128), F32)

    @pl.when(gz == nz - 1)
    def _():
        E[:, :, 10:12] = jnp.zeros((2, 2, 2, 32, 128), F32)

    @pl.when(gy == 0)
    def _():
        E[:, :, :, 0:8] = jnp.zeros((2, 2, 12, 8, 128), F32)

    @pl.when(gy == ny - 1)
    def _():
        E[:, :, :, 24:32] = jnp.zeros((2, 2, 12, 8, 128), F32)

    def coarse(zc, row_groups, tiles):
        for rows in row_groups:
            mid = pl.ds(rows, 8)
            near, centre = [], []
            for c in range(2):
                main, ext = E[c, 0, zc, mid], E[c, 1, zc, mid]
                side = across(main, ext, 2, tiles)
                centre.append([main, ext])
                near.append(
                    [
                        side[t]
                        + (E[c, t, zc - 1, mid] + E[c, t, zc + 1, mid])
                        + (E[c, t, zc, pl.ds(rows - 2, 8)] + E[c, t, zc, pl.ds(rows + 2, 8)])
                        for t in range(tiles)
                    ]
                )
            for t in range(tiles):
                wr, wi = G[0, t, zc, mid], G[1, t, zc, mid]
                E1[0, t, zc, mid] = 1.5 * centre[0][t] + (wr * near[0][t] - wi * near[1][t])
                E1[1, t, zc, mid] = 1.5 * centre[1][t] + (wr * near[1][t] + wi * near[0][t])

    def own_planes(zc, carry):
        coarse(zc, (8, 16), 2)
        coarse(zc, (4, 20), 1)
        return carry

    lax.fori_loop(2, 10, own_planes, 0, unroll=4)
    coarse(1, (8, 16), 1)
    coarse(10, (8, 16), 1)

    def correct(zc, carry):
        carry = list(carry)
        for yh in range(2):
            rows = 8 + 8 * yh
            mid, out = pl.ds(rows, 8), slice(8 * yh, 8 * yh + 8)
            e, base = [], []
            for c in range(2):
                main = E1[c, 0, zc + 2, mid]
                side = across(main, E1[c, 1, zc + 2, mid], 1, 1)[0]
                e.append(main)
                base.append(
                    main + side + (E1[c, 0, zc + 2, pl.ds(rows - 1, 8)] + E1[c, 0, zc + 2, pl.ds(rows + 1, 8)])
                )
            for k in range(2):
                z = 2 * zc + k
                dr, di = D[0, z, out], D[1, z, out]
                rr = RP[0, z, out] + (base[0] + E1[0, 0, zc + 1 + 2 * k, mid]) - (dr * e[0] - di * e[1])
                ri = RP[1, z, out] + (base[1] + E1[1, 0, zc + 1 + 2 * k, mid]) - (dr * e[1] + di * e[0])
                carry[0] = carry[0] + (rr * rr + ri * ri)
                ar = B[0, 0, z + 4, mid] + e[0]
                ai = B[1, 0, z + 4, mid] + e[1]
                ADJ[0, z, out] = ar
                ADJ[1, z, out] = ai
                fr, fi = FW[0, z, out], FW[1, z, out]
                pr = fr * ar - fi * ai
                pi = fr * ai + fi * ar
                label = LI[z, out]
                for m in range(NMAT):
                    chosen = label == m
                    carry[1 + m] = carry[1 + m] + jnp.where(chosen, pr, 0.0)
                    carry[9 + m] = carry[9 + m] + jnp.where(chosen, pi, 0.0)
        return tuple(carry)

    sums = lax.fori_loop(0, 8, correct, (zero,) * 17, unroll=2)
    store = pltpu.make_async_copy(ADJ, adj_hbm, local_sem.at[0])
    store.start()

    pl.semaphore_wait(ready.at[2], met)

    ordered = list(sums[1:]) + [src_sq, pre_sq, sums[0]]
    ACC[...] = jnp.zeros((24, 128), F32)
    for k, value in enumerate(ordered):
        ACC[k : k + 1] = jnp.sum(value, axis=0, keepdims=True)
    totals = jnp.sum(ACC[...], axis=1, keepdims=True)
    lane24 = lax.broadcasted_iota(jnp.int32, (24, 128), 1)
    row24 = lax.broadcasted_iota(jnp.int32, (24, 128), 0)
    row = jnp.sum(jnp.where(lane24 == row24, totals, 0.0), axis=0, keepdims=True)

    for stage, (peers, slots, own) in enumerate(((y_peers, R1, gy), (xz_peers, R2, gx * nz + gz))):
        count = len(peers)
        VAL[stage] = row
        for offset in peers:
            pltpu.make_async_remote_copy(
                src_ref=VAL.at[stage],
                dst_ref=slots.at[own],
                send_sem=send_r.at[stage],
                recv_sem=recv_r.at[stage],
                device_id=device(offset),
                device_id_type=MESH,
            ).start()
        slots[own] = row
        every = pltpu.make_async_remote_copy(
            src_ref=slots.at[pl.ds(0, count)],
            dst_ref=slots.at[pl.ds(0, count)],
            send_sem=send_r.at[stage],
            recv_sem=recv_r.at[stage],
            device_id=device(peers[0]),
            device_id_type=MESH,
        )
        every.wait_recv()
        every.wait_send()
        row = slots[0]
        for k in range(1, count + 1):
            row = row + slots[k]

    cells = float(nx * ny * nz * 16 * 16 * 128)
    one = lax.broadcasted_iota(jnp.int32, (1, 128), 1)
    row_ref[...] = jnp.where(one < 2 * NMAT, (-KH2 / cells**0.5) * row, jnp.sqrt(jnp.maximum(row, 0.0) / cells))
    store.wait()


def finish(adjoint, row_ref, out, grad, norms):
    out[...] = adjoint[...]
    row = row_ref[...]
    grad[0:1] = row[:, :NMAT]
    grad[1:2] = pltpu.roll(row, 128 - NMAT, 1)[:, :NMAT]
    norms[...] = pltpu.roll(row, 128 - 2 * NMAT, 1)[0, :3]


def shards(sizes, source, adjoint_guess, forward_field, labels, perm_real, perm_imag):
    vmem = lambda *shape: pltpu.VMEM(shape, F32)
    dma = pltpu.SemaphoreType.DMA
    n_a, n_c = 50, 18
    adjoint, row = pl.pallas_call(
        functools.partial(kernel, sizes),
        out_shape=(
            jax.ShapeDtypeStruct(adjoint_guess.shape, F32),
            jax.ShapeDtypeStruct((1, 128), F32),
        ),
        in_specs=[pl.BlockSpec(memory_space=pltpu.HBM)] * 4 + [pl.BlockSpec(memory_space=pltpu.SMEM)] * 2,
        out_specs=(pl.BlockSpec(memory_space=pltpu.HBM), pl.BlockSpec(memory_space=pltpu.VMEM)),
        scratch_shapes=[
            vmem(5, 2, 24, 32, 128),
            vmem(2, 2, 24, 32, 128),
            vmem(2, 2, 24, 32, 128),
            vmem(2, 16, 16, 128),
            vmem(2, 16, 16, 128),
            pltpu.VMEM((16, 16, 128), jnp.int32),
            vmem(2, 16, 16, 128),
            vmem(2, 2, 12, 32, 128),
            vmem(2, 2, 12, 32, 128),
            vmem(2, 2, 12, 32, 128),
            vmem(2, 16, 16, 128),
            vmem(16, 16, 128),
            vmem(5, 8, 8, 128),
            vmem(4, 2, 8, 128),
            vmem(2, 8, 128),
            vmem(2, 8, 128),
            vmem(2, 8, 128),
            vmem(2, 6, 4, 8, 128),
            vmem(2, 3, 4, 8, 128),
            vmem(2, 2, 8, 128),
            vmem(2, 3, 4, 8, 128),
            vmem(24, 128),
            vmem(2, 1, 128),
            vmem(sizes[1], 1, 128),
            vmem(sizes[0] * sizes[2], 1, 128),
            dma((4,)),
            dma((n_a,)),
            dma((n_a,)),
            dma((n_c,)),
            dma((n_c,)),
            dma((2,)),
            dma((2,)),
            pltpu.SemaphoreType.REGULAR((3,)),
        ],
        compiler_params=pltpu.CompilerParams(collective_id=0, has_side_effects=True, vmem_limit_bytes=60 << 20),
    )(adjoint_guess, source, forward_field, labels, perm_real, perm_imag)
    return pl.pallas_call(
        finish,
        out_shape=(
            jax.ShapeDtypeStruct(adjoint_guess.shape, F32),
            jax.ShapeDtypeStruct((2, NMAT), F32),
            jax.ShapeDtypeStruct((3,), F32),
        ),
        in_specs=[pl.BlockSpec(memory_space=pltpu.VMEM)] * 2,
        out_specs=(pl.BlockSpec(memory_space=pltpu.VMEM),) * 3,
    )(adjoint, row)


def solution(mesh):
    sizes = tuple(mesh.shape[a] for a in AXES)
    field = P(None, "gz", "gy", "gx")
    return jax.shard_map(
        functools.partial(shards, sizes),
        mesh=mesh,
        in_specs=(field, field, field, P("gz", "gy", "gx"), P(), P()),
        out_specs=(field, P(), P()),
        check_vma=False,
    )
```

```python
import functools

import jax
import jax.numpy as jnp
from jax import lax
from jax.experimental import pallas as pl
from jax.experimental.pallas import tpu as pltpu
from jax.sharding import PartitionSpec as P

MESH = pl.DeviceIdType.MESH
NMAT = 8
KH2 = 0.5
SHIFT = 0.5
F32 = jnp.float32
AXES = ("gx", "gy", "gz")


def near_offsets():
    return [
        (dx, dy, dz)
        for dx in (-1, 0, 1)
        for dy in (-1, 0, 1)
        for dz in (-1, 0, 1)
        if (dx, dy, dz) != (0, 0, 0)
    ]


def kernel(
    sizes,
    guess_hbm,
    source_hbm,
    forward_hbm,
    labels_hbm,
    pr_ref,
    pi_ref,
    adj_hbm,
    row_ref,
    F,
    B,
    H,
    D,
    FW,
    LI,
    RP,
    E,
    E1,
    G,
    ADJ,
    ER,
    TB,
    PU,
    PL,
    PG,
    PE,
    PZ,
    RU,
    RL,
    RZ,
    RG,
    RE,
    ACC,
    VAL,
    R1,
    R2,
    local_sem,
    send_a,
    recv_a,
    send_c,
    recv_c,
    send_r,
    recv_r,
    ready,
):
    nx, ny, nz = sizes
    gx, gy, gz = (lax.axis_index(a) for a in AXES)

    def device(offset):
        dx, dy, dz = offset
        return {
            "gx": lax.rem(gx + (dx % nx), nx),
            "gy": lax.rem(gy + (dy % ny), ny),
            "gz": lax.rem(gz + (dz % nz), nz),
        }

    loads = [
        pltpu.make_async_copy(labels_hbm, LI, local_sem.at[0]),
        pltpu.make_async_copy(guess_hbm, F.at[0:2, 0, pl.ds(4, 16), pl.ds(8, 16)], local_sem.at[1]),
        pltpu.make_async_copy(source_hbm, F.at[2:4, 0, pl.ds(4, 16), pl.ds(8, 16)], local_sem.at[2]),
        pltpu.make_async_copy(forward_hbm, FW, local_sem.at[3]),
    ]
    for copy in loads:
        copy.start()

    y_peers = [(0, dy, 0) for dy in range(1, ny)]
    xz_peers = [(dx, 0, dz) for dx in range(nx) for dz in range(nz) if (dx, dz) != (0, 0)]

    y_peers.sort(key=lambda o: -min(o[1], ny - o[1]))
    xz_peers.sort(key=lambda o: -(min(o[0], nx - o[0]) + min(o[2], nz - o[2])))

    def greet(semaphore, offsets):
        offsets = {(dx % nx, dy % ny, dz % nz) for dx, dy, dz in offsets}
        for offset in sorted(offsets):
            pl.semaphore_signal(semaphore, inc=1, device_id=device(offset), device_id_type=MESH)
        return len(offsets)

    barrier = pltpu.get_barrier_semaphore()
    met = greet(barrier, near_offsets())

    lane = lax.broadcasted_iota(jnp.int32, (8, 128), 1)
    row8 = lax.broadcasted_iota(jnp.int32, (8, 128), 0)
    even_lane = lane % 2 == 0
    even_row = row8 % 2 == 0
    left_half = lane % 8 < 4
    slot_of = lane // 8
    left_ok = (gx > 0).astype(F32)
    right_ok = (gx < nx - 1).astype(F32)
    side_ok = jnp.where(lane < 64, right_ok, left_ok)
    slot_ok = jnp.where(left_half, left_ok, right_ok)
    low_y_ok, high_y_ok = (gy > 0).astype(F32), (gy < ny - 1).astype(F32)
    low_z_ok, high_z_ok = (gz > 0).astype(F32), (gz < nz - 1).astype(F32)
    halo_rows_ok = jnp.where(row8 < 4, high_y_ok, low_y_ok)

    for m in range(NMAT):
        er = jnp.full((8, 128), pr_ref[m], F32)
        ei = jnp.full((8, 128), pi_ref[m], F32)
        dr = 6.0 - KH2 * (er + SHIFT * ei)
        di = -KH2 * (SHIFT * er - ei)
        half = 0.5 / (dr * dr + di * di)
        TB[0, m] = dr * half
        TB[1, m] = -di * half
        TB[2, m] = dr
        TB[3, m] = di
        TB[4, m] = er

    def look_up(label, tables):
        high = label >= 3.5
        rest = jnp.where(high, label - 4.0, label)
        middle = rest >= 1.5
        odd = jnp.where(middle, rest - 2.0, rest) >= 0.5
        out = []
        for t in tables:
            pairs = [jnp.where(odd, TB[t, 2 * i + 1], TB[t, 2 * i]) for i in range(4)]
            quads = [jnp.where(middle, pairs[2 * i + 1], pairs[2 * i]) for i in range(2)]
            out.append(jnp.where(high, quads[1], quads[0]))
        return out

    def block_sum(v):
        v = v + jnp.where(even_row, pltpu.roll(v, 7, 0), pltpu.roll(v, 1, 0))
        return v + jnp.where(even_lane, pltpu.roll(v, 127, 1), pltpu.roll(v, 1, 1))

    loads[0].wait()

    def own_coefficients(z, carry):
        for yh in range(2):
            label = LI[z, 8 * yh : 8 * yh + 8].astype(F32)
            F[4, 0, z + 4, 8 + 8 * yh : 16 + 8 * yh] = label
            hr, hi, dr, di, er = look_up(label, (0, 1, 2, 3, 4))
            H[0, 0, z + 4, 8 + 8 * yh : 16 + 8 * yh] = hr
            H[1, 0, z + 4, 8 + 8 * yh : 16 + 8 * yh] = hi
            D[0, z, 8 * yh : 8 * yh + 8] = dr
            D[1, z, 8 * yh : 8 * yh + 8] = di
            ER[z, 8 * yh : 8 * yh + 8] = er
        return carry

    lax.fori_loop(0, 16, own_coefficients, 0, unroll=4)

    def own_coarse(zc, carry):
        for yh in range(2):
            rows = slice(8 * yh, 8 * yh + 8)
            q4 = (KH2 * 4.0 / 8.0) * block_sum(ER[2 * zc, rows] + ER[2 * zc + 1, rows])
            scale = 0.5 / (36.0 + q4 * q4)
            G[0, 0, zc + 2, 8 + 8 * yh : 16 + 8 * yh] = 6.0 * scale
            G[1, 0, zc + 2, 8 + 8 * yh : 16 + 8 * yh] = -q4 * scale
        return carry

    lax.fori_loop(0, 8, own_coarse, 0, unroll=4)

    def pack(pieces):
        total = jnp.zeros((8, 128), F32)
        for slot, piece in enumerate(pieces):
            total = jnp.where(slot_of == slot, pltpu.roll(piece, (8 * slot + 4) % 128, 1), total)
        return total

    for yh in range(2):
        rows = slice(8 + 8 * yh, 16 + 8 * yh)
        PL[yh] = pack([F[4, 0, 4 + z, rows] for z in range(16)])
        PG[yh] = pack([G[c, 0, 2 + z, rows] for c in range(2) for z in range(8)])
    loads[1].wait()
    loads[2].wait()

    def pack_quarter(zq, carry):
        for yh in range(2):
            rows = slice(8 + 8 * yh, 16 + 8 * yh)
            PU[zq, yh] = pack([F[f, 0, 4 + 4 * zq + p, rows] for f in range(4) for p in range(4)])
        return carry

    lax.fori_loop(0, 4, pack_quarter, 0, unroll=2)
    edge_slots = [(0, 3), (1, 3), (2, 2), (3, 2), (4, 2)]
    for up in range(2):
        for yh in range(2):
            rows = slice(8 + 8 * yh, 16 + 8 * yh)
            PZ[up, yh] = pack(
                [F[f, 0, (20 - deep + p) if up else 4 + p, rows] for f, deep in edge_slots for p in range(deep)]
            )

    def planes(dz, own, deep, at):
        if dz == 0:
            return pl.ds(at, own), pl.ds(at, own)
        if dz > 0:
            return pl.ds(at + own - deep, deep), pl.ds(at - deep, deep)
        return pl.ds(at, deep), pl.ds(at + own, deep)

    started = []

    def send(offset, source, target, sends, receives):
        k = len(started)
        copy = pltpu.make_async_remote_copy(
            src_ref=source,
            dst_ref=target,
            send_sem=sends.at[k],
            recv_sem=receives.at[k],
            device_id=device(offset),
            device_id_type=MESH,
        )
        copy.start()
        started.append(copy)

    pl.semaphore_wait(barrier, met)

    def tiles(dy):
        if dy == 0:
            return pl.ds(0, 2), pl.ds(0, 2), pl.ds(0, 8)
        if dy > 0:
            return pl.ds(1, 1), pl.ds(2, 1), pl.ds(4, 4)
        return pl.ds(0, 1), pl.ds(2, 1), pl.ds(0, 4)

    def send_fine(offset):
        dx, dy, dz = offset
        if dx == 0:
            for fields, deep in ((pl.ds(0, 2), 4), (pl.ds(2, 3), 3)):
                deep = deep - 1 if dy and dz else deep
                from_z, to_z = planes(dz, 16, deep, 4)
                from_y, to_y = planes(dy, 16, deep, 8)
                send(offset, F.at[fields, 0, from_z, from_y], F.at[fields, 0, to_z, to_y], send_a, recv_a)
            return
        side = 0 if dx > 0 else 1
        from_y, to_y, rows = tiles(dy)
        if dz:
            up = 1 if dz > 0 else 0
            send(offset, PZ.at[up, from_y, rows], RZ.at[side, 1 - up, to_y, rows], send_a, recv_a)
        else:
            send(offset, PU.at[:, from_y, rows], RU.at[side, :, to_y, rows], send_a, recv_a)
            send(offset, PL.at[from_y, rows], RL.at[side, to_y, rows], send_a, recv_a)

    for offset in sorted(near_offsets(), key=lambda o: (o[:2] != (0, 0), -sum(abs(d) for d in o))):
        send_fine(offset)
    for offset in ((0, 0, 1), (0, 0, -1), (0, 1, 0), (0, -1, 0)):
        from_z, to_z = planes(offset[2], 8, 1, 2)
        from_y, to_y = planes(offset[1], 16, 4, 8)
        send(offset, G.at[:, 0, from_z, from_y], G.at[:, 0, to_z, to_y], send_a, recv_a)
    for offset in ((1, 0, 0), (-1, 0, 0)):
        send(offset, PG, RG.at[0 if offset[0] > 0 else 1], send_a, recv_a)

    met = greet(ready.at[0], [o for o in near_offsets() if o[1] == 0 or (o[0], o[2]) == (0, 0)])

    for copy in started:
        copy.wait()
    loads[3].wait()
    pl.semaphore_wait(ready.at[0], met)
    met = greet(ready.at[1], [(2, 0, 0), (-2, 0, 0), (0, 2, 0), (0, -2, 0)])

    def merged(low, high):
        return jnp.where(left_half, low, high) * slot_ok

    def spread(ref, index, tile, value):
        if tile < 2:
            ref[(*index, slice(8 + 8 * tile, 16 + 8 * tile))] = value
        else:
            ref[(*index, slice(24, 28))] = value[0:4]
            ref[(*index, slice(4, 8))] = value[4:8]

    def from_slot(packed, slot):
        return pltpu.roll(packed, (124 - 8 * slot) % 128, 1)

    for up in range(2):
        for tile in range(3):
            both = merged(RZ[0, up, tile], RZ[1, up, tile])
            ok = side_ok * (high_z_ok if up else low_z_ok)
            ok = ok * halo_rows_ok if tile == 2 else ok
            slot = 0
            for f, deep in edge_slots:
                for p in range(deep):
                    at = 20 + p if up else 4 - deep + p
                    piece = from_slot(both, slot)
                    slot += 1
                    if f < 4:
                        spread(F, (f, 1, at), tile, piece)
                    else:
                        hr, hi = look_up(piece, (0, 1))
                        spread(H, (0, 1, at), tile, hr * ok)
                        spread(H, (1, 1, at), tile, hi * ok)
        for p in range(3):
            at = 20 + p if up else 1 + p
            ok = high_z_ok if up else low_z_ok
            for yg, y_ok in enumerate((low_y_ok, 1.0, 1.0, high_y_ok)):
                rows = slice(8 * yg, 8 * yg + 8)
                hr, hi = look_up(F[4, 0, at, rows], (0, 1))
                H[0, 0, at, rows] = hr * (ok * y_ok)
                H[1, 0, at, rows] = hi * (ok * y_ok)

    def unpack_quarter(zq, carry):
        for tile in range(3):
            both = merged(RU[0, zq, tile], RU[1, zq, tile])
            for f in range(4):
                for p in range(4):
                    spread(F, (f, 1, 4 + 4 * zq + p), tile, from_slot(both, 4 * f + p))
        return carry

    lax.fori_loop(0, 4, unpack_quarter, 0, unroll=4)

    def halo_coefficients(z, carry):
        shift = 124 - 8 * (z - 4)
        for tile in range(3):
            hr, hi = look_up(pltpu.roll(merged(RL[0, tile], RL[1, tile]), shift, 1), (0, 1))
            ok = side_ok * halo_rows_ok if tile == 2 else side_ok
            spread(H, (0, 1, z), tile, hr * ok)
            spread(H, (1, 1, z), tile, hi * ok)
        for rows, ok in ((slice(0, 8), low_y_ok), (slice(24, 32), high_y_ok)):
            hr, hi = look_up(F[4, 0, z, rows], (0, 1))
            H[0, 0, z, rows] = hr * ok
            H[1, 0, z, rows] = hi * ok
        return carry

    lax.fori_loop(4, 20, halo_coefficients, 0, unroll=8)

    @pl.when(gz == 0)
    def _():
        F[0:2, :, 0:4] = jnp.zeros((2, 2, 4, 32, 128), F32)
        G[:, 0, 1] = jnp.zeros((2, 32, 128), F32)

    @pl.when(gz == nz - 1)
    def _():
        F[0:2, :, 20:24] = jnp.zeros((2, 2, 4, 32, 128), F32)
        G[:, 0, 10] = jnp.zeros((2, 32, 128), F32)

    @pl.when(gy == 0)
    def _():
        F[0:2, :, :, 4:8] = jnp.zeros((2, 2, 24, 4, 128), F32)
        G[:, 0, :, 4:8] = jnp.zeros((2, 12, 4, 128), F32)

    @pl.when(gy == ny - 1)
    def _():
        F[0:2, :, :, 24:28] = jnp.zeros((2, 2, 24, 4, 128), F32)
        G[:, 0, :, 24:28] = jnp.zeros((2, 12, 4, 128), F32)

    for yh in range(2):
        both = merged(RG[0, yh], RG[1, yh])
        for c in range(2):
            for z in range(8):
                G[c, 1, 2 + z, 8 + 8 * yh : 16 + 8 * yh] = pltpu.roll(both, (124 - 8 * (8 * c + z)) % 128, 1)

    def across(main, ext, step, tiles):
        at = lax.broadcasted_iota(jnp.int32, main.shape, 1)
        low, high = at < step, at >= 128 - step
        ml, el = pltpu.roll(main, step, 1), pltpu.roll(ext, step, 1)
        mr, er = pltpu.roll(main, 128 - step, 1), pltpu.roll(ext, 128 - step, 1)
        out = [jnp.where(low, el, ml) + jnp.where(high, er, mr)]
        if tiles == 2:
            out.append(jnp.where(low, ml, el) + jnp.where(high, mr, er))
        return out

    def sweep(source, target, first, last):
        def plane(z, carry):
            for rows in (4, 12, 20):
                mid = pl.ds(rows, 8)
                near = [[None, None], [None, None]]
                centre = [[None, None], [None, None]]
                for c in range(2):
                    main, ext = source[c, 0, z, mid], source[c, 1, z, mid]
                    centre[c] = [main, ext]
                    side = across(main, ext, 1, 2)
                    for t in range(2):
                        near[c][t] = (
                            side[t]
                            + (source[c, t, z - 1, mid] + source[c, t, z + 1, mid])
                            + (source[c, t, z, pl.ds(rows - 1, 8)] + source[c, t, z, pl.ds(rows + 1, 8)])
                        )
                for t in range(2):
                    wr = F[2, t, z, mid] + near[0][t]
                    wi = F[3, t, z, mid] + near[1][t]
                    hr, hi = H[0, t, z, mid], H[1, t, z, mid]
                    target[0, t, z, mid] = 0.5 * centre[0][t] + (hr * wr - hi * wi)
                    target[1, t, z, mid] = 0.5 * centre[1][t] + (hr * wi + hi * wr)
            return carry

        lax.fori_loop(first, last, plane, 0, unroll=(last - first) // 2)

    sweep(F, B, 1, 23)
    sweep(B, F, 2, 22)
    sweep(F, B, 3, 21)

    pl.semaphore_wait(ready.at[1], met)
    met = greet(ready.at[2], [(0, 4, 0), (0, -4, 0)])

    zero = jnp.zeros((8, 128), F32)

    def residual(zc, carry):
        src_sq, pre_sq = carry
        for yh in range(2):
            rows = 8 + 8 * yh
            mid, out = pl.ds(rows, 8), slice(8 * yh, 8 * yh + 8)
            sums = [zero, zero]
            for k in range(2):
                z = 2 * zc + k
                near, centre = [], []
                for c in range(2):
                    main = B[c, 0, z + 4, mid]
                    centre.append(main)
                    side = across(main, B[c, 1, z + 4, mid], 1, 1)[0]
                    near.append(
                        side
                        + (B[c, 0, z + 3, mid] + B[c, 0, z + 5, mid])
                        + (B[c, 0, z + 4, pl.ds(rows - 1, 8)] + B[c, 0, z + 4, pl.ds(rows + 1, 8)])
                    )
                dr, di = D[0, z, out], D[1, z, out]
                sr, si = F[2, 0, z + 4, mid], F[3, 0, z + 4, mid]
                rr = sr + near[0] - (dr * centre[0] - di * centre[1])
                ri = si + near[1] - (dr * centre[1] + di * centre[0])
                RP[0, z, out] = rr
                RP[1, z, out] = ri
                src_sq = src_sq + (sr * sr + si * si)
                pre_sq = pre_sq + (rr * rr + ri * ri)
                sums = [sums[0] + rr, sums[1] + ri]
            br, bi = 0.5 * block_sum(sums[0]), 0.5 * block_sum(sums[1])
            wr, wi = G[0, 0, zc + 2, mid], G[1, 0, zc + 2, mid]
            E[0, 0, zc + 2, mid] = wr * br - wi * bi
            E[1, 0, zc + 2, mid] = wr * bi + wi * br
        return src_sq, pre_sq

    src_sq, pre_sq = lax.fori_loop(0, 8, residual, (zero, zero), unroll=4)

    for yh in range(2):
        PE[yh] = pack([E[c, 0, 2 + z, 8 + 8 * yh : 16 + 8 * yh] for c in range(2) for z in range(8)])
    del started[:]
    for offset in near_offsets():
        dx, dy, dz = offset
        if dx and dy and dz:
            continue
        if dx == 0:
            from_z, to_z = planes(dz, 8, 1 if dy else 2, 2)
            from_y, to_y = planes(dy, 16, 4, 8)
            send(offset, E.at[:, 0, from_z, from_y], E.at[:, 0, to_z, to_y], send_c, recv_c)
        else:
            side = 0 if dx > 0 else 1
            from_y, to_y, rows = tiles(dy)
            send(offset, PE.at[from_y, rows], RE.at[side, 1 - dz, to_y, rows], send_c, recv_c)
    for copy in started:
        copy.wait()

    for part, where in ((1, range(8)), (0, (7,)), (2, (0,))):
        for tile in range(3 if part == 1 else 2):
            both = merged(RE[0, part, tile], RE[1, part, tile])
            for c in range(2):
                for z in where:
                    at = 2 + z if part == 1 else (1 if part == 0 else 10)
                    spread(E, (c, 1, at), tile, from_slot(both, 8 * c + z))

    @pl.when(gz == 0)
    def _():
        E[:, :, 0:2] = jnp.zeros((2, 2, 2, 32, 128), F32)

    @pl.when(gz == nz - 1)
    def _():
        E[:, :, 10:12] = jnp.zeros((2, 2, 2, 32, 128), F32)

    @pl.when(gy == 0)
    def _():
        E[:, :, :, 4:8] = jnp.zeros((2, 2, 12, 4, 128), F32)

    @pl.when(gy == ny - 1)
    def _():
        E[:, :, :, 24:28] = jnp.zeros((2, 2, 12, 4, 128), F32)

    def coarse(zc, row_groups, tiles):
        for rows in row_groups:
            mid = pl.ds(rows, 8)
            near, centre = [], []
            for c in range(2):
                main, ext = E[c, 0, zc, mid], E[c, 1, zc, mid]
                side = across(main, ext, 2, tiles)
                centre.append([main, ext])
                near.append(
                    [
                        side[t]
                        + (E[c, t, zc - 1, mid] + E[c, t, zc + 1, mid])
                        + (E[c, t, zc, pl.ds(rows - 2, 8)] + E[c, t, zc, pl.ds(rows + 2, 8)])
                        for t in range(tiles)
                    ]
                )
            for t in range(tiles):
                wr, wi = G[0, t, zc, mid], G[1, t, zc, mid]
                E1[0, t, zc, mid] = 1.5 * centre[0][t] + (wr * near[0][t] - wi * near[1][t])
                E1[1, t, zc, mid] = 1.5 * centre[1][t] + (wr * near[1][t] + wi * near[0][t])

    def own_planes(zc, carry):
        coarse(zc, (8, 16), 2)
        coarse(zc, (4, 20), 1)
        return carry

    lax.fori_loop(2, 10, own_planes, 0, unroll=4)
    coarse(1, (8, 16), 1)
    coarse(10, (8, 16), 1)

    def correct(zc, carry):
        carry = list(carry)
        for yh in range(2):
            rows = 8 + 8 * yh
            mid, out = pl.ds(rows, 8), slice(8 * yh, 8 * yh + 8)
            e, base = [], []
            for c in range(2):
                main = E1[c, 0, zc + 2, mid]
                side = across(main, E1[c, 1, zc + 2, mid], 1, 1)[0]
                e.append(main)
                base.append(
                    main + side + (E1[c, 0, zc + 2, pl.ds(rows - 1, 8)] + E1[c, 0, zc + 2, pl.ds(rows + 1, 8)])
                )
            for k in range(2):
                z = 2 * zc + k
                dr, di = D[0, z, out], D[1, z, out]
                rr = RP[0, z, out] + (base[0] + E1[0, 0, zc + 1 + 2 * k, mid]) - (dr * e[0] - di * e[1])
                ri = RP[1, z, out] + (base[1] + E1[1, 0, zc + 1 + 2 * k, mid]) - (dr * e[1] + di * e[0])
                carry[0] = carry[0] + (rr * rr + ri * ri)
                ar = B[0, 0, z + 4, mid] + e[0]
                ai = B[1, 0, z + 4, mid] + e[1]
                ADJ[0, z, out] = ar
                ADJ[1, z, out] = ai
                fr, fi = FW[0, z, out], FW[1, z, out]
                pr = fr * ar - fi * ai
                pi = fr * ai + fi * ar
                label = LI[z, out]
                for m in range(NMAT):
                    chosen = label == m
                    carry[1 + m] = carry[1 + m] + jnp.where(chosen, pr, 0.0)
                    carry[9 + m] = carry[9 + m] + jnp.where(chosen, pi, 0.0)
        return tuple(carry)

    sums = lax.fori_loop(0, 8, correct, (zero,) * 17, unroll=2)
    store = pltpu.make_async_copy(ADJ, adj_hbm, local_sem.at[0])
    store.start()

    pl.semaphore_wait(ready.at[2], met)

    ordered = list(sums[1:]) + [src_sq, pre_sq, sums[0]]
    ACC[...] = jnp.zeros((24, 128), F32)
    for k, value in enumerate(ordered):
        ACC[k : k + 1] = jnp.sum(value, axis=0, keepdims=True)
    totals = jnp.sum(ACC[...], axis=1, keepdims=True)
    lane24 = lax.broadcasted_iota(jnp.int32, (24, 128), 1)
    row24 = lax.broadcasted_iota(jnp.int32, (24, 128), 0)
    row = jnp.sum(jnp.where(lane24 == row24, totals, 0.0), axis=0, keepdims=True)

    for stage, (peers, slots, own) in enumerate(((y_peers, R1, gy), (xz_peers, R2, gx * nz + gz))):
        count = len(peers)
        VAL[stage] = row
        for offset in peers:
            pltpu.make_async_remote_copy(
                src_ref=VAL.at[stage],
                dst_ref=slots.at[own],
                send_sem=send_r.at[stage],
                recv_sem=recv_r.at[stage],
                device_id=device(offset),
                device_id_type=MESH,
            ).start()
        slots[own] = row
        every = pltpu.make_async_remote_copy(
            src_ref=slots.at[pl.ds(0, count)],
            dst_ref=slots.at[pl.ds(0, count)],
            send_sem=send_r.at[stage],
            recv_sem=recv_r.at[stage],
            device_id=device(peers[0]),
            device_id_type=MESH,
        )
        every.wait_recv()
        every.wait_send()
        row = slots[0]
        for k in range(1, count + 1):
            row = row + slots[k]

    cells = float(nx * ny * nz * 16 * 16 * 128)
    one = lax.broadcasted_iota(jnp.int32, (1, 128), 1)
    row_ref[...] = jnp.where(one < 2 * NMAT, (-KH2 / cells**0.5) * row, jnp.sqrt(jnp.maximum(row, 0.0) / cells))
    store.wait()


def finish(adjoint, row_ref, out, grad, norms):
    out[...] = adjoint[...]
    row = row_ref[...]
    grad[0:1] = row[:, :NMAT]
    grad[1:2] = pltpu.roll(row, 128 - NMAT, 1)[:, :NMAT]
    norms[...] = pltpu.roll(row, 128 - 2 * NMAT, 1)[0, :3]


def shards(sizes, source, adjoint_guess, forward_field, labels, perm_real, perm_imag):
    vmem = lambda *shape: pltpu.VMEM(shape, F32)
    dma = pltpu.SemaphoreType.DMA
    n_a, n_c = 50, 18
    adjoint, row = pl.pallas_call(
        functools.partial(kernel, sizes),
        out_shape=(
            jax.ShapeDtypeStruct(adjoint_guess.shape, F32),
            jax.ShapeDtypeStruct((1, 128), F32),
        ),
        in_specs=[pl.BlockSpec(memory_space=pltpu.HBM)] * 4 + [pl.BlockSpec(memory_space=pltpu.SMEM)] * 2,
        out_specs=(pl.BlockSpec(memory_space=pltpu.HBM), pl.BlockSpec(memory_space=pltpu.VMEM)),
        scratch_shapes=[
            vmem(5, 2, 24, 32, 128),
            vmem(2, 2, 24, 32, 128),
            vmem(2, 2, 24, 32, 128),
            vmem(2, 16, 16, 128),
            vmem(2, 16, 16, 128),
            pltpu.VMEM((16, 16, 128), jnp.int32),
            vmem(2, 16, 16, 128),
            vmem(2, 2, 12, 32, 128),
            vmem(2, 2, 12, 32, 128),
            vmem(2, 2, 12, 32, 128),
            vmem(2, 16, 16, 128),
            vmem(16, 16, 128),
            vmem(5, 8, 8, 128),
            vmem(4, 2, 8, 128),
            vmem(2, 8, 128),
            vmem(2, 8, 128),
            vmem(2, 8, 128),
            vmem(2, 2, 8, 128),
            vmem(2, 4, 3, 8, 128),
            vmem(2, 3, 8, 128),
            vmem(2, 2, 3, 8, 128),
            vmem(2, 2, 8, 128),
            vmem(2, 3, 3, 8, 128),
            vmem(24, 128),
            vmem(2, 1, 128),
            vmem(sizes[1], 1, 128),
            vmem(sizes[0] * sizes[2], 1, 128),
            dma((4,)),
            dma((n_a,)),
            dma((n_a,)),
            dma((n_c,)),
            dma((n_c,)),
            dma((2,)),
            dma((2,)),
            pltpu.SemaphoreType.REGULAR((3,)),
        ],
        compiler_params=pltpu.CompilerParams(collective_id=0, has_side_effects=True, vmem_limit_bytes=60 << 20),
    )(adjoint_guess, source, forward_field, labels, perm_real, perm_imag)
    return pl.pallas_call(
        finish,
        out_shape=(
            jax.ShapeDtypeStruct(adjoint_guess.shape, F32),
            jax.ShapeDtypeStruct((2, NMAT), F32),
            jax.ShapeDtypeStruct((3,), F32),
        ),
        in_specs=[pl.BlockSpec(memory_space=pltpu.VMEM)] * 2,
        out_specs=(pl.BlockSpec(memory_space=pltpu.VMEM),) * 3,
    )(adjoint, row)


def solution(mesh):
    sizes = tuple(mesh.shape[a] for a in AXES)
    field = P(None, "gz", "gy", "gx")
    return jax.shard_map(
        functools.partial(shards, sizes),
        mesh=mesh,
        in_specs=(field, field, field, P("gz", "gy", "gx"), P(), P()),
        out_specs=(field, P(), P()),
        check_vma=False,
    )
```

```python
import functools

import jax
import jax.numpy as jnp
from jax import lax
from jax.experimental import pallas as pl
from jax.experimental.pallas import tpu as pltpu
from jax.sharding import PartitionSpec as P

MESH = pl.DeviceIdType.MESH
NMAT = 8
KH2 = 0.5
SHIFT = 0.5
F32 = jnp.float32
AXES = ("gx", "gy", "gz")


def near_offsets():
    return [
        (dx, dy, dz)
        for dx in (-1, 0, 1)
        for dy in (-1, 0, 1)
        for dz in (-1, 0, 1)
        if (dx, dy, dz) != (0, 0, 0)
    ]


def kernel(
    sizes,
    guess_hbm,
    source_hbm,
    forward_hbm,
    labels_hbm,
    pr_ref,
    pi_ref,
    adj_hbm,
    row_ref,
    F,
    B,
    H,
    D,
    FW,
    LI,
    RP,
    E,
    E1,
    G,
    ADJ,
    ER,
    TB,
    PU,
    PL,
    PG,
    PE,
    PZ,
    RU,
    RL,
    RZ,
    RG,
    RE,
    ACC,
    VAL,
    R1,
    R2,
    local_sem,
    send_a,
    recv_a,
    send_c,
    recv_c,
    send_r,
    recv_r,
    ready,
):
    nx, ny, nz = sizes
    gx, gy, gz = (lax.axis_index(a) for a in AXES)

    def device(offset):
        dx, dy, dz = offset
        return {
            "gx": lax.rem(gx + (dx % nx), nx),
            "gy": lax.rem(gy + (dy % ny), ny),
            "gz": lax.rem(gz + (dz % nz), nz),
        }

    loads = [
        pltpu.make_async_copy(labels_hbm, LI, local_sem.at[0]),
        pltpu.make_async_copy(guess_hbm, F.at[0:2, 0, pl.ds(4, 16), pl.ds(8, 16)], local_sem.at[1]),
        pltpu.make_async_copy(source_hbm, F.at[2:4, 0, pl.ds(4, 16), pl.ds(8, 16)], local_sem.at[2]),
        pltpu.make_async_copy(forward_hbm, FW, local_sem.at[3]),
    ]
    for copy in loads:
        copy.start()

    y_peers = [(0, dy, 0) for dy in range(1, ny)]
    xz_peers = [(dx, 0, dz) for dx in range(nx) for dz in range(nz) if (dx, dz) != (0, 0)]

    y_peers.sort(key=lambda o: -min(o[1], ny - o[1]))
    xz_peers.sort(key=lambda o: -(min(o[0], nx - o[0]) + min(o[2], nz - o[2])))

    def greet(semaphore, offsets):
        offsets = {(dx % nx, dy % ny, dz % nz) for dx, dy, dz in offsets}
        for offset in sorted(offsets):
            pl.semaphore_signal(semaphore, inc=1, device_id=device(offset), device_id_type=MESH)
        return len(offsets)

    barrier = pltpu.get_barrier_semaphore()
    met = greet(barrier, near_offsets())

    lane = lax.broadcasted_iota(jnp.int32, (8, 128), 1)
    row8 = lax.broadcasted_iota(jnp.int32, (8, 128), 0)
    even_lane = lane % 2 == 0
    even_row = row8 % 2 == 0
    left_half = lane % 8 < 4
    slot_of = lane // 8
    left_ok = (gx > 0).astype(F32)
    right_ok = (gx < nx - 1).astype(F32)
    side_ok = jnp.where(lane < 64, right_ok, left_ok)
    slot_ok = jnp.where(left_half, left_ok, right_ok)
    low_y_ok, high_y_ok = (gy > 0).astype(F32), (gy < ny - 1).astype(F32)
    low_z_ok, high_z_ok = (gz > 0).astype(F32), (gz < nz - 1).astype(F32)
    halo_rows_ok = jnp.where(row8 < 4, high_y_ok, low_y_ok)

    def look_up(label, tables):
        high = label >= 3.5
        rest = jnp.where(high, label - 4.0, label)
        middle = rest >= 1.5
        odd = jnp.where(middle, rest - 2.0, rest) >= 0.5
        out = []
        for t in tables:
            pairs = [jnp.where(odd, TB[t, 2 * i + 1], TB[t, 2 * i]) for i in range(4)]
            quads = [jnp.where(middle, pairs[2 * i + 1], pairs[2 * i]) for i in range(2)]
            out.append(jnp.where(high, quads[1], quads[0]))
        return out

    def block_sum(v):
        v = v + jnp.where(even_row, pltpu.roll(v, 7, 0), pltpu.roll(v, 1, 0))
        return v + jnp.where(even_lane, pltpu.roll(v, 127, 1), pltpu.roll(v, 1, 1))

    loads[0].wait()
    F[4, 0, 4:20, 8:24] = LI[...].astype(F32)

    def pack(pieces):
        total = jnp.zeros((8, 128), F32)
        for slot, piece in enumerate(pieces):
            total = jnp.where(slot_of == slot, pltpu.roll(piece, (8 * slot + 4) % 128, 1), total)
        return total

    for yh in range(2):
        rows = slice(8 + 8 * yh, 16 + 8 * yh)
        PL[yh] = pack([F[4, 0, 4 + z, rows] for z in range(16)])
    loads[1].wait()
    loads[2].wait()

    def pack_quarter(zq, carry):
        for yh in range(2):
            rows = slice(8 + 8 * yh, 16 + 8 * yh)
            PU[zq, yh] = pack([F[f, 0, 4 + 4 * zq + p, rows] for f in range(4) for p in range(4)])
        return carry

    lax.fori_loop(0, 4, pack_quarter, 0, unroll=2)
    edge_slots = [(0, 3), (1, 3), (2, 2), (3, 2), (4, 2)]
    for up in range(2):
        for yh in range(2):
            rows = slice(8 + 8 * yh, 16 + 8 * yh)
            PZ[up, yh] = pack(
                [F[f, 0, (20 - deep + p) if up else 4 + p, rows] for f, deep in edge_slots for p in range(deep)]
            )

    def planes(dz, own, deep, at):
        if dz == 0:
            return pl.ds(at, own), pl.ds(at, own)
        if dz > 0:
            return pl.ds(at + own - deep, deep), pl.ds(at - deep, deep)
        return pl.ds(at, deep), pl.ds(at + own, deep)

    started = []

    def send(offset, source, target, sends, receives):
        k = len(started)
        copy = pltpu.make_async_remote_copy(
            src_ref=source,
            dst_ref=target,
            send_sem=sends.at[k],
            recv_sem=receives.at[k],
            device_id=device(offset),
            device_id_type=MESH,
        )
        copy.start()
        started.append(copy)

    pl.semaphore_wait(barrier, met)

    def tiles(dy):
        if dy == 0:
            return pl.ds(0, 2), pl.ds(0, 2), pl.ds(0, 8)
        if dy > 0:
            return pl.ds(1, 1), pl.ds(2, 1), pl.ds(4, 4)
        return pl.ds(0, 1), pl.ds(2, 1), pl.ds(0, 4)

    def send_fine(offset, parts):
        dx, dy, dz = offset
        if dx == 0:
            for fields, deep in parts:
                deep = deep - 1 if dy and dz else deep
                from_z, to_z = planes(dz, 16, deep, 4)
                from_y, to_y = planes(dy, 16, deep, 8)
                send(offset, F.at[fields, 0, from_z, from_y], F.at[fields, 0, to_z, to_y], send_a, recv_a)
            return
        side = 0 if dx > 0 else 1
        from_y, to_y, rows = tiles(dy)
        if len(parts) == 2:
            if dz == 0:
                send(offset, PU.at[:, from_y, rows], RU.at[side, :, to_y, rows], send_a, recv_a)
        elif dz == 0:
            send(offset, PL.at[from_y, rows], RL.at[side, to_y, rows], send_a, recv_a)
        else:
            up = 1 if dz > 0 else 0
            send(offset, PZ.at[up, from_y, rows], RZ.at[side, 1 - up, to_y, rows], send_a, recv_a)

    order = sorted(near_offsets(), key=lambda o: (o[:2] != (0, 0), -sum(abs(d) for d in o)))
    for offset in order:
        send_fine(offset, [(pl.ds(4, 1), 3)])
    first_group = list(started)
    for offset in order:
        send_fine(offset, [(pl.ds(0, 2), 4), (pl.ds(2, 2), 3)])

    for m in range(NMAT):
        er = jnp.full((8, 128), pr_ref[m], F32)
        ei = jnp.full((8, 128), pi_ref[m], F32)
        dr = 6.0 - KH2 * (er + SHIFT * ei)
        di = -KH2 * (SHIFT * er - ei)
        half = 0.5 / (dr * dr + di * di)
        TB[0, m] = dr * half
        TB[1, m] = -di * half
        TB[2, m] = dr
        TB[3, m] = di
        TB[4, m] = er

    def own_coefficients(z, carry):
        for yh in range(2):
            label = F[4, 0, z + 4, 8 + 8 * yh : 16 + 8 * yh]
            hr, hi, dr, di, er = look_up(label, (0, 1, 2, 3, 4))
            H[0, 0, z + 4, 8 + 8 * yh : 16 + 8 * yh] = hr
            H[1, 0, z + 4, 8 + 8 * yh : 16 + 8 * yh] = hi
            D[0, z, 8 * yh : 8 * yh + 8] = dr
            D[1, z, 8 * yh : 8 * yh + 8] = di
            ER[z, 8 * yh : 8 * yh + 8] = er
        return carry

    lax.fori_loop(0, 16, own_coefficients, 0, unroll=4)

    def own_coarse(zc, carry):
        for yh in range(2):
            rows = slice(8 * yh, 8 * yh + 8)
            q4 = (KH2 * 4.0 / 8.0) * block_sum(ER[2 * zc, rows] + ER[2 * zc + 1, rows])
            scale = 0.5 / (36.0 + q4 * q4)
            G[0, 0, zc + 2, 8 + 8 * yh : 16 + 8 * yh] = 6.0 * scale
            G[1, 0, zc + 2, 8 + 8 * yh : 16 + 8 * yh] = -q4 * scale
        return carry

    lax.fori_loop(0, 8, own_coarse, 0, unroll=4)

    for yh in range(2):
        rows = slice(8 + 8 * yh, 16 + 8 * yh)
        PG[yh] = pack([G[c, 0, 2 + z, rows] for c in range(2) for z in range(8)])
    for offset in ((0, 0, 1), (0, 0, -1), (0, 1, 0), (0, -1, 0)):
        from_z, to_z = planes(offset[2], 8, 1, 2)
        from_y, to_y = planes(offset[1], 16, 4, 8)
        send(offset, G.at[:, 0, from_z, from_y], G.at[:, 0, to_z, to_y], send_a, recv_a)
    for offset in ((1, 0, 0), (-1, 0, 0)):
        send(offset, PG, RG.at[0 if offset[0] > 0 else 1], send_a, recv_a)

    met = greet(ready.at[0], [o for o in near_offsets() if o[1] == 0 or (o[0], o[2]) == (0, 0)])

    for copy in first_group:
        copy.wait()

    def merged(low, high):
        return jnp.where(left_half, low, high) * slot_ok

    def spread(ref, index, tile, value):
        if tile < 2:
            ref[(*index, slice(8 + 8 * tile, 16 + 8 * tile))] = value
        else:
            ref[(*index, slice(24, 28))] = value[0:4]
            ref[(*index, slice(4, 8))] = value[4:8]

    def from_slot(packed, slot):
        return pltpu.roll(packed, (124 - 8 * slot) % 128, 1)

    for up in range(2):
        for tile in range(3):
            both = merged(RZ[0, up, tile], RZ[1, up, tile])
            ok = side_ok * (high_z_ok if up else low_z_ok)
            ok = ok * halo_rows_ok if tile == 2 else ok
            slot = 0
            for f, deep in edge_slots:
                for p in range(deep):
                    at = 20 + p if up else 4 - deep + p
                    piece = from_slot(both, slot)
                    slot += 1
                    if f < 4:
                        spread(F, (f, 1, at), tile, piece)
                    else:
                        hr, hi = look_up(piece, (0, 1))
                        spread(H, (0, 1, at), tile, hr * ok)
                        spread(H, (1, 1, at), tile, hi * ok)
        for p in range(3):
            at = 20 + p if up else 1 + p
            ok = high_z_ok if up else low_z_ok
            for yg, y_ok in enumerate((low_y_ok, 1.0, 1.0, high_y_ok)):
                rows = slice(8 * yg, 8 * yg + 8)
                hr, hi = look_up(F[4, 0, at, rows], (0, 1))
                H[0, 0, at, rows] = hr * (ok * y_ok)
                H[1, 0, at, rows] = hi * (ok * y_ok)

    def halo_coefficients(z, carry):
        shift = 124 - 8 * (z - 4)
        for tile in range(3):
            hr, hi = look_up(pltpu.roll(merged(RL[0, tile], RL[1, tile]), shift, 1), (0, 1))
            ok = side_ok * halo_rows_ok if tile == 2 else side_ok
            spread(H, (0, 1, z), tile, hr * ok)
            spread(H, (1, 1, z), tile, hi * ok)
        for rows, ok in ((slice(0, 8), low_y_ok), (slice(24, 32), high_y_ok)):
            hr, hi = look_up(F[4, 0, z, rows], (0, 1))
            H[0, 0, z, rows] = hr * ok
            H[1, 0, z, rows] = hi * ok
        return carry

    lax.fori_loop(4, 20, halo_coefficients, 0, unroll=8)

    for copy in started[len(first_group) :]:
        copy.wait()
    loads[3].wait()

    def unpack_quarter(zq, carry):
        for tile in range(3):
            both = merged(RU[0, zq, tile], RU[1, zq, tile])
            for f in range(4):
                for p in range(4):
                    spread(F, (f, 1, 4 + 4 * zq + p), tile, from_slot(both, 4 * f + p))
        return carry

    lax.fori_loop(0, 4, unpack_quarter, 0, unroll=4)

    pl.semaphore_wait(ready.at[0], met)
    met = greet(ready.at[1], [(2, 0, 0), (-2, 0, 0), (0, 2, 0), (0, -2, 0)])

    @pl.when(gz == 0)
    def _():
        F[0:2, :, 0:4] = jnp.zeros((2, 2, 4, 32, 128), F32)
        G[:, 0, 1] = jnp.zeros((2, 32, 128), F32)

    @pl.when(gz == nz - 1)
    def _():
        F[0:2, :, 20:24] = jnp.zeros((2, 2, 4, 32, 128), F32)
        G[:, 0, 10] = jnp.zeros((2, 32, 128), F32)

    @pl.when(gy == 0)
    def _():
        F[0:2, :, :, 4:8] = jnp.zeros((2, 2, 24, 4, 128), F32)
        G[:, 0, :, 4:8] = jnp.zeros((2, 12, 4, 128), F32)

    @pl.when(gy == ny - 1)
    def _():
        F[0:2, :, :, 24:28] = jnp.zeros((2, 2, 24, 4, 128), F32)
        G[:, 0, :, 24:28] = jnp.zeros((2, 12, 4, 128), F32)

    for yh in range(2):
        both = merged(RG[0, yh], RG[1, yh])
        for c in range(2):
            for z in range(8):
                G[c, 1, 2 + z, 8 + 8 * yh : 16 + 8 * yh] = pltpu.roll(both, (124 - 8 * (8 * c + z)) % 128, 1)

    def across(main, ext, step, tiles):
        at = lax.broadcasted_iota(jnp.int32, main.shape, 1)
        low, high = at < step, at >= 128 - step
        ml, el = pltpu.roll(main, step, 1), pltpu.roll(ext, step, 1)
        mr, er = pltpu.roll(main, 128 - step, 1), pltpu.roll(ext, 128 - step, 1)
        out = [jnp.where(low, el, ml) + jnp.where(high, er, mr)]
        if tiles == 2:
            out.append(jnp.where(low, ml, el) + jnp.where(high, mr, er))
        return out

    def sweep(source, target, first, last):
        def plane(z, carry):
            for rows in (4, 12, 20):
                mid = pl.ds(rows, 8)
                near = [[None, None], [None, None]]
                centre = [[None, None], [None, None]]
                for c in range(2):
                    main, ext = source[c, 0, z, mid], source[c, 1, z, mid]
                    centre[c] = [main, ext]
                    side = across(main, ext, 1, 2)
                    for t in range(2):
                        near[c][t] = (
                            side[t]
                            + (source[c, t, z - 1, mid] + source[c, t, z + 1, mid])
                            + (source[c, t, z, pl.ds(rows - 1, 8)] + source[c, t, z, pl.ds(rows + 1, 8)])
                        )
                for t in range(2):
                    wr = F[2, t, z, mid] + near[0][t]
                    wi = F[3, t, z, mid] + near[1][t]
                    hr, hi = H[0, t, z, mid], H[1, t, z, mid]
                    target[0, t, z, mid] = 0.5 * centre[0][t] + (hr * wr - hi * wi)
                    target[1, t, z, mid] = 0.5 * centre[1][t] + (hr * wi + hi * wr)
            return carry

        lax.fori_loop(first, last, plane, 0, unroll=(last - first) // 2)

    sweep(F, B, 1, 23)
    sweep(B, F, 2, 22)
    sweep(F, B, 3, 21)

    pl.semaphore_wait(ready.at[1], met)
    met = greet(ready.at[2], [(0, 4, 0), (0, -4, 0)])

    zero = jnp.zeros((8, 128), F32)

    def residual(zc, carry):
        src_sq, pre_sq = carry
        for yh in range(2):
            rows = 8 + 8 * yh
            mid, out = pl.ds(rows, 8), slice(8 * yh, 8 * yh + 8)
            sums = [zero, zero]
            for k in range(2):
                z = 2 * zc + k
                near, centre = [], []
                for c in range(2):
                    main = B[c, 0, z + 4, mid]
                    centre.append(main)
                    side = across(main, B[c, 1, z + 4, mid], 1, 1)[0]
                    near.append(
                        side
                        + (B[c, 0, z + 3, mid] + B[c, 0, z + 5, mid])
                        + (B[c, 0, z + 4, pl.ds(rows - 1, 8)] + B[c, 0, z + 4, pl.ds(rows + 1, 8)])
                    )
                dr, di = D[0, z, out], D[1, z, out]
                sr, si = F[2, 0, z + 4, mid], F[3, 0, z + 4, mid]
                rr = sr + near[0] - (dr * centre[0] - di * centre[1])
                ri = si + near[1] - (dr * centre[1] + di * centre[0])
                RP[0, z, out] = rr
                RP[1, z, out] = ri
                src_sq = src_sq + (sr * sr + si * si)
                pre_sq = pre_sq + (rr * rr + ri * ri)
                sums = [sums[0] + rr, sums[1] + ri]
            br, bi = 0.5 * block_sum(sums[0]), 0.5 * block_sum(sums[1])
            wr, wi = G[0, 0, zc + 2, mid], G[1, 0, zc + 2, mid]
            E[0, 0, zc + 2, mid] = wr * br - wi * bi
            E[1, 0, zc + 2, mid] = wr * bi + wi * br
        return src_sq, pre_sq

    src_sq, pre_sq = lax.fori_loop(0, 8, residual, (zero, zero), unroll=4)

    for yh in range(2):
        PE[yh] = pack([E[c, 0, 2 + z, 8 + 8 * yh : 16 + 8 * yh] for c in range(2) for z in range(8)])
    del started[:]
    for offset in near_offsets():
        dx, dy, dz = offset
        if dx and dy and dz:
            continue
        if dx == 0:
            from_z, to_z = planes(dz, 8, 1 if dy else 2, 2)
            from_y, to_y = planes(dy, 16, 4, 8)
            send(offset, E.at[:, 0, from_z, from_y], E.at[:, 0, to_z, to_y], send_c, recv_c)
        else:
            side = 0 if dx > 0 else 1
            from_y, to_y, rows = tiles(dy)
            send(offset, PE.at[from_y, rows], RE.at[side, 1 - dz, to_y, rows], send_c, recv_c)
    for copy in started:
        copy.wait()

    for part, where in ((1, range(8)), (0, (7,)), (2, (0,))):
        for tile in range(3 if part == 1 else 2):
            both = merged(RE[0, part, tile], RE[1, part, tile])
            for c in range(2):
                for z in where:
                    at = 2 + z if part == 1 else (1 if part == 0 else 10)
                    spread(E, (c, 1, at), tile, from_slot(both, 8 * c + z))

    @pl.when(gz == 0)
    def _():
        E[:, :, 0:2] = jnp.zeros((2, 2, 2, 32, 128), F32)

    @pl.when(gz == nz - 1)
    def _():
        E[:, :, 10:12] = jnp.zeros((2, 2, 2, 32, 128), F32)

    @pl.when(gy == 0)
    def _():
        E[:, :, :, 4:8] = jnp.zeros((2, 2, 12, 4, 128), F32)

    @pl.when(gy == ny - 1)
    def _():
        E[:, :, :, 24:28] = jnp.zeros((2, 2, 12, 4, 128), F32)

    def coarse(zc, row_groups, tiles):
        for rows in row_groups:
            mid = pl.ds(rows, 8)
            near, centre = [], []
            for c in range(2):
                main, ext = E[c, 0, zc, mid], E[c, 1, zc, mid]
                side = across(main, ext, 2, tiles)
                centre.append([main, ext])
                near.append(
                    [
                        side[t]
                        + (E[c, t, zc - 1, mid] + E[c, t, zc + 1, mid])
                        + (E[c, t, zc, pl.ds(rows - 2, 8)] + E[c, t, zc, pl.ds(rows + 2, 8)])
                        for t in range(tiles)
                    ]
                )
            for t in range(tiles):
                wr, wi = G[0, t, zc, mid], G[1, t, zc, mid]
                E1[0, t, zc, mid] = 1.5 * centre[0][t] + (wr * near[0][t] - wi * near[1][t])
                E1[1, t, zc, mid] = 1.5 * centre[1][t] + (wr * near[1][t] + wi * near[0][t])

    def own_planes(zc, carry):
        coarse(zc, (8, 16), 2)
        coarse(zc, (4, 20), 1)
        return carry

    lax.fori_loop(2, 10, own_planes, 0, unroll=4)
    coarse(1, (8, 16), 1)
    coarse(10, (8, 16), 1)

    def correct(zc, carry):
        carry = list(carry)
        for yh in range(2):
            rows = 8 + 8 * yh
            mid, out = pl.ds(rows, 8), slice(8 * yh, 8 * yh + 8)
            e, base = [], []
            for c in range(2):
                main = E1[c, 0, zc + 2, mid]
                side = across(main, E1[c, 1, zc + 2, mid], 1, 1)[0]
                e.append(main)
                base.append(
                    main + side + (E1[c, 0, zc + 2, pl.ds(rows - 1, 8)] + E1[c, 0, zc + 2, pl.ds(rows + 1, 8)])
                )
            for k in range(2):
                z = 2 * zc + k
                dr, di = D[0, z, out], D[1, z, out]
                rr = RP[0, z, out] + (base[0] + E1[0, 0, zc + 1 + 2 * k, mid]) - (dr * e[0] - di * e[1])
                ri = RP[1, z, out] + (base[1] + E1[1, 0, zc + 1 + 2 * k, mid]) - (dr * e[1] + di * e[0])
                carry[0] = carry[0] + (rr * rr + ri * ri)
                ar = B[0, 0, z + 4, mid] + e[0]
                ai = B[1, 0, z + 4, mid] + e[1]
                ADJ[0, z, out] = ar
                ADJ[1, z, out] = ai
                fr, fi = FW[0, z, out], FW[1, z, out]
                pr = fr * ar - fi * ai
                pi = fr * ai + fi * ar
                label = LI[z, out]
                for m in range(NMAT):
                    chosen = label == m
                    carry[1 + m] = carry[1 + m] + jnp.where(chosen, pr, 0.0)
                    carry[9 + m] = carry[9 + m] + jnp.where(chosen, pi, 0.0)
        return tuple(carry)

    sums = lax.fori_loop(0, 8, correct, (zero,) * 17, unroll=2)
    store = pltpu.make_async_copy(ADJ, adj_hbm, local_sem.at[0])
    store.start()

    pl.semaphore_wait(ready.at[2], met)

    ordered = list(sums[1:]) + [src_sq, pre_sq, sums[0]]
    ACC[...] = jnp.zeros((24, 128), F32)
    for k, value in enumerate(ordered):
        ACC[k : k + 1] = jnp.sum(value, axis=0, keepdims=True)
    totals = jnp.sum(ACC[...], axis=1, keepdims=True)
    lane24 = lax.broadcasted_iota(jnp.int32, (24, 128), 1)
    row24 = lax.broadcasted_iota(jnp.int32, (24, 128), 0)
    row = jnp.sum(jnp.where(lane24 == row24, totals, 0.0), axis=0, keepdims=True)

    for stage, (peers, slots, own) in enumerate(((y_peers, R1, gy), (xz_peers, R2, gx * nz + gz))):
        count = len(peers)
        VAL[stage] = row
        for offset in peers:
            pltpu.make_async_remote_copy(
                src_ref=VAL.at[stage],
                dst_ref=slots.at[own],
                send_sem=send_r.at[stage],
                recv_sem=recv_r.at[stage],
                device_id=device(offset),
                device_id_type=MESH,
            ).start()
        slots[own] = row
        every = pltpu.make_async_remote_copy(
            src_ref=slots.at[pl.ds(0, count)],
            dst_ref=slots.at[pl.ds(0, count)],
            send_sem=send_r.at[stage],
            recv_sem=recv_r.at[stage],
            device_id=device(peers[0]),
            device_id_type=MESH,
        )
        every.wait_recv()
        every.wait_send()
        row = slots[0]
        for k in range(1, count + 1):
            row = row + slots[k]

    cells = float(nx * ny * nz * 16 * 16 * 128)
    one = lax.broadcasted_iota(jnp.int32, (1, 128), 1)
    row_ref[...] = jnp.where(one < 2 * NMAT, (-KH2 / cells**0.5) * row, jnp.sqrt(jnp.maximum(row, 0.0) / cells))
    store.wait()


def finish(adjoint, row_ref, out, grad, norms):
    out[...] = adjoint[...]
    row = row_ref[...]
    grad[0:1] = row[:, :NMAT]
    grad[1:2] = pltpu.roll(row, 128 - NMAT, 1)[:, :NMAT]
    norms[...] = pltpu.roll(row, 128 - 2 * NMAT, 1)[0, :3]


def shards(sizes, source, adjoint_guess, forward_field, labels, perm_real, perm_imag):
    vmem = lambda *shape: pltpu.VMEM(shape, F32)
    dma = pltpu.SemaphoreType.DMA
    n_a, n_c = 54, 18
    adjoint, row = pl.pallas_call(
        functools.partial(kernel, sizes),
        out_shape=(
            jax.ShapeDtypeStruct(adjoint_guess.shape, F32),
            jax.ShapeDtypeStruct((1, 128), F32),
        ),
        in_specs=[pl.BlockSpec(memory_space=pltpu.HBM)] * 4 + [pl.BlockSpec(memory_space=pltpu.SMEM)] * 2,
        out_specs=(pl.BlockSpec(memory_space=pltpu.HBM), pl.BlockSpec(memory_space=pltpu.VMEM)),
        scratch_shapes=[
            vmem(5, 2, 24, 32, 128),
            vmem(2, 2, 24, 32, 128),
            vmem(2, 2, 24, 32, 128),
            vmem(2, 16, 16, 128),
            vmem(2, 16, 16, 128),
            pltpu.VMEM((16, 16, 128), jnp.int32),
            vmem(2, 16, 16, 128),
            vmem(2, 2, 12, 32, 128),
            vmem(2, 2, 12, 32, 128),
            vmem(2, 2, 12, 32, 128),
            vmem(2, 16, 16, 128),
            vmem(16, 16, 128),
            vmem(5, 8, 8, 128),
            vmem(4, 2, 8, 128),
            vmem(2, 8, 128),
            vmem(2, 8, 128),
            vmem(2, 8, 128),
            vmem(2, 2, 8, 128),
            vmem(2, 4, 3, 8, 128),
            vmem(2, 3, 8, 128),
            vmem(2, 2, 3, 8, 128),
            vmem(2, 2, 8, 128),
            vmem(2, 3, 3, 8, 128),
            vmem(24, 128),
            vmem(2, 1, 128),
            vmem(sizes[1], 1, 128),
            vmem(sizes[0] * sizes[2], 1, 128),
            dma((4,)),
            dma((n_a,)),
            dma((n_a,)),
            dma((n_c,)),
            dma((n_c,)),
            dma((2,)),
            dma((2,)),
            pltpu.SemaphoreType.REGULAR((3,)),
        ],
        compiler_params=pltpu.CompilerParams(collective_id=0, has_side_effects=True, vmem_limit_bytes=20 << 20),
    )(*(pltpu.with_memory_space_constraint(a, pltpu.HBM) for a in (adjoint_guess, source, forward_field, labels, perm_real, perm_imag)))
    return pl.pallas_call(
        finish,
        out_shape=(
            jax.ShapeDtypeStruct(adjoint_guess.shape, F32),
            jax.ShapeDtypeStruct((2, NMAT), F32),
            jax.ShapeDtypeStruct((3,), F32),
        ),
        in_specs=[pl.BlockSpec(memory_space=pltpu.VMEM)] * 2,
        out_specs=(pl.BlockSpec(memory_space=pltpu.VMEM),) * 3,
    )(*(pltpu.with_memory_space_constraint(a, pltpu.VMEM) for a in (adjoint, row)))


def solution(mesh):
    sizes = tuple(mesh.shape[a] for a in AXES)
    field = P(None, "gz", "gy", "gx")
    return jax.shard_map(
        functools.partial(shards, sizes),
        mesh=mesh,
        in_specs=(field, field, field, P("gz", "gy", "gx"), P(), P()),
        out_specs=(field, P(), P()),
        check_vma=False,
    )
```

```python
import functools

import jax
import jax.numpy as jnp
from jax import lax
from jax.experimental import pallas as pl
from jax.experimental.pallas import tpu as pltpu
from jax.sharding import PartitionSpec as P

MESH = pl.DeviceIdType.MESH
NMAT = 8
KH2 = 0.5
SHIFT = 0.5
F32 = jnp.float32
AXES = ("gx", "gy", "gz")


def near_offsets():
    return [
        (dx, dy, dz)
        for dx in (-1, 0, 1)
        for dy in (-1, 0, 1)
        for dz in (-1, 0, 1)
        if (dx, dy, dz) != (0, 0, 0)
    ]


def kernel(
    sizes,
    guess_hbm,
    source_hbm,
    forward_hbm,
    labels_hbm,
    pr_ref,
    pi_ref,
    adj_hbm,
    row_ref,
    F,
    B,
    H,
    D,
    FW,
    LI,
    RP,
    E,
    E1,
    G,
    ADJ,
    ER,
    TB,
    PU,
    PL,
    PG,
    PE,
    PZ,
    RU,
    RL,
    RZ,
    RG,
    RE,
    ACC,
    VAL,
    R1,
    R2,
    local_sem,
    send_a,
    recv_a,
    send_c,
    recv_c,
    send_r,
    recv_r,
    ready,
):
    nx, ny, nz = sizes
    gx, gy, gz = (lax.axis_index(a) for a in AXES)

    def device(offset):
        dx, dy, dz = offset
        return {
            "gx": lax.rem(gx + (dx % nx), nx),
            "gy": lax.rem(gy + (dy % ny), ny),
            "gz": lax.rem(gz + (dz % nz), nz),
        }

    loads = [
        pltpu.make_async_copy(labels_hbm, LI, local_sem.at[0]),
        pltpu.make_async_copy(guess_hbm, F.at[0:2, 0, pl.ds(4, 16), pl.ds(8, 16)], local_sem.at[1]),
        pltpu.make_async_copy(source_hbm, F.at[2:4, 0, pl.ds(4, 16), pl.ds(8, 16)], local_sem.at[2]),
        pltpu.make_async_copy(forward_hbm, FW, local_sem.at[3]),
    ]
    for copy in loads:
        copy.start()

    y_peers = [(0, dy, 0) for dy in range(1, ny)]
    xz_peers = [(dx, 0, dz) for dx in range(nx) for dz in range(nz) if (dx, dz) != (0, 0)]

    y_peers.sort(key=lambda o: -min(o[1], ny - o[1]))
    xz_peers.sort(key=lambda o: -(min(o[0], nx - o[0]) + min(o[2], nz - o[2])))

    def greet(semaphore, offsets):
        offsets = {(dx % nx, dy % ny, dz % nz) for dx, dy, dz in offsets}
        for offset in sorted(offsets):
            pl.semaphore_signal(semaphore, inc=1, device_id=device(offset), device_id_type=MESH)
        return len(offsets)

    barrier = pltpu.get_barrier_semaphore()
    met = greet(barrier, near_offsets())

    lane = lax.broadcasted_iota(jnp.int32, (8, 128), 1)
    row8 = lax.broadcasted_iota(jnp.int32, (8, 128), 0)
    even_lane = lane % 2 == 0
    even_row = row8 % 2 == 0
    left_half = lane % 8 < 4
    slot_of = lane // 8
    left_ok = (gx > 0).astype(F32)
    right_ok = (gx < nx - 1).astype(F32)
    side_ok = jnp.where(lane < 64, right_ok, left_ok)
    slot_ok = jnp.where(left_half, left_ok, right_ok)
    low_y_ok, high_y_ok = (gy > 0).astype(F32), (gy < ny - 1).astype(F32)
    low_z_ok, high_z_ok = (gz > 0).astype(F32), (gz < nz - 1).astype(F32)
    halo_rows_ok = jnp.where(row8 < 4, high_y_ok, low_y_ok)

    def look_up(label, tables):
        high = label >= 3.5
        rest = jnp.where(high, label - 4.0, label)
        middle = rest >= 1.5
        odd = jnp.where(middle, rest - 2.0, rest) >= 0.5
        out = []
        for t in tables:
            pairs = [jnp.where(odd, TB[t, 2 * i + 1], TB[t, 2 * i]) for i in range(4)]
            quads = [jnp.where(middle, pairs[2 * i + 1], pairs[2 * i]) for i in range(2)]
            out.append(jnp.where(high, quads[1], quads[0]))
        return out

    def block_sum(v):
        v = v + jnp.where(even_row, pltpu.roll(v, 7, 0), pltpu.roll(v, 1, 0))
        return v + jnp.where(even_lane, pltpu.roll(v, 127, 1), pltpu.roll(v, 1, 1))

    loads[0].wait()
    F[4, 0, 4:20, 8:24] = LI[...].astype(F32)

    def pack(pieces):
        total = jnp.zeros((8, 128), F32)
        for slot, piece in enumerate(pieces):
            total = jnp.where(slot_of == slot, pltpu.roll(piece, (8 * slot + 4) % 128, 1), total)
        return total

    for yh in range(2):
        rows = slice(8 + 8 * yh, 16 + 8 * yh)
        PL[yh] = pack([F[4, 0, 4 + z, rows] for z in range(16)])
    loads[1].wait()
    loads[2].wait()

    def pack_quarter(zq, carry):
        for yh in range(2):
            rows = slice(8 + 8 * yh, 16 + 8 * yh)
            PU[zq, yh] = pack([F[f, 0, 4 + 4 * zq + p, rows] for f in range(4) for p in range(4)])
        return carry

    lax.fori_loop(0, 4, pack_quarter, 0, unroll=2)
    edge_slots = [(0, 3), (1, 3), (2, 2), (3, 2), (4, 2)]
    for up in range(2):
        for yh in range(2):
            rows = slice(8 + 8 * yh, 16 + 8 * yh)
            PZ[up, yh] = pack(
                [F[f, 0, (20 - deep + p) if up else 4 + p, rows] for f, deep in edge_slots for p in range(deep)]
            )

    def planes(dz, own, deep, at):
        if dz == 0:
            return pl.ds(at, own), pl.ds(at, own)
        if dz > 0:
            return pl.ds(at + own - deep, deep), pl.ds(at - deep, deep)
        return pl.ds(at, deep), pl.ds(at + own, deep)

    started = []

    def send(offset, source, target, sends, receives):
        k = len(started)
        copy = pltpu.make_async_remote_copy(
            src_ref=source,
            dst_ref=target,
            send_sem=sends.at[k],
            recv_sem=receives.at[k],
            device_id=device(offset),
            device_id_type=MESH,
        )
        copy.start()
        started.append(copy)

    pl.semaphore_wait(barrier, met)

    def tiles(dy):
        if dy == 0:
            return pl.ds(0, 2), pl.ds(0, 2), pl.ds(0, 8)
        if dy > 0:
            return pl.ds(1, 1), pl.ds(2, 1), pl.ds(4, 4)
        return pl.ds(0, 1), pl.ds(2, 1), pl.ds(0, 4)

    def send_fine(offset, parts):
        dx, dy, dz = offset
        if dx == 0:
            for fields, deep in parts:
                deep = deep - 1 if dy and dz else deep
                from_z, to_z = planes(dz, 16, deep, 4)
                from_y, to_y = planes(dy, 16, deep, 8)
                send(offset, F.at[fields, 0, from_z, from_y], F.at[fields, 0, to_z, to_y], send_a, recv_a)
            return
        side = 0 if dx > 0 else 1
        from_y, to_y, rows = tiles(dy)
        if len(parts) == 2:
            if dz == 0:
                send(offset, PU.at[:, from_y, rows], RU.at[side, :, to_y, rows], send_a, recv_a)
        elif dz == 0:
            send(offset, PL.at[from_y, rows], RL.at[side, to_y, rows], send_a, recv_a)
        else:
            up = 1 if dz > 0 else 0
            send(offset, PZ.at[up, from_y, rows], RZ.at[side, 1 - up, to_y, rows], send_a, recv_a)

    order = sorted(near_offsets(), key=lambda o: (o[:2] != (0, 0), -sum(abs(d) for d in o)))
    for offset in order:
        send_fine(offset, [(pl.ds(4, 1), 3)])
    first_group = list(started)
    for offset in order:
        send_fine(offset, [(pl.ds(0, 2), 4), (pl.ds(2, 2), 3)])

    for m in range(NMAT):
        er = jnp.full((8, 128), pr_ref[m], F32)
        ei = jnp.full((8, 128), pi_ref[m], F32)
        dr = 6.0 - KH2 * (er + SHIFT * ei)
        di = -KH2 * (SHIFT * er - ei)
        half = 0.5 / (dr * dr + di * di)
        TB[0, m] = dr * half
        TB[1, m] = -di * half
        TB[2, m] = dr
        TB[3, m] = di
        TB[4, m] = er

    def own_coefficients(z, carry):
        for yh in range(2):
            label = F[4, 0, z + 4, 8 + 8 * yh : 16 + 8 * yh]
            hr, hi, dr, di, er = look_up(label, (0, 1, 2, 3, 4))
            H[0, 0, z + 4, 8 + 8 * yh : 16 + 8 * yh] = hr
            H[1, 0, z + 4, 8 + 8 * yh : 16 + 8 * yh] = hi
            D[0, z, 8 * yh : 8 * yh + 8] = dr
            D[1, z, 8 * yh : 8 * yh + 8] = di
            ER[z, 8 * yh : 8 * yh + 8] = er
        return carry

    lax.fori_loop(0, 16, own_coefficients, 0, unroll=4)

    def own_coarse(zc, carry):
        for yh in range(2):
            rows = slice(8 * yh, 8 * yh + 8)
            q4 = (KH2 * 4.0 / 8.0) * block_sum(ER[2 * zc, rows] + ER[2 * zc + 1, rows])
            scale = 0.5 / (36.0 + q4 * q4)
            G[0, 0, zc + 2, 8 + 8 * yh : 16 + 8 * yh] = 6.0 * scale
            G[1, 0, zc + 2, 8 + 8 * yh : 16 + 8 * yh] = -q4 * scale
        return carry

    lax.fori_loop(0, 8, own_coarse, 0, unroll=4)

    for yh in range(2):
        rows = slice(8 + 8 * yh, 16 + 8 * yh)
        PG[yh] = pack([G[c, 0, 2 + z, rows] for c in range(2) for z in range(8)])
    for offset in ((0, 0, 1), (0, 0, -1), (0, 1, 0), (0, -1, 0)):
        from_z, to_z = planes(offset[2], 8, 1, 2)
        from_y, to_y = planes(offset[1], 16, 4, 8)
        send(offset, G.at[:, 0, from_z, from_y], G.at[:, 0, to_z, to_y], send_a, recv_a)
    for offset in ((1, 0, 0), (-1, 0, 0)):
        send(offset, PG, RG.at[0 if offset[0] > 0 else 1], send_a, recv_a)

    met = greet(ready.at[0], [o for o in near_offsets() if o[1] == 0 or (o[0], o[2]) == (0, 0)])

    for copy in first_group:
        copy.wait()

    def merged(low, high):
        return jnp.where(left_half, low, high) * slot_ok

    def spread(ref, index, tile, value):
        if tile < 2:
            ref[(*index, slice(8 + 8 * tile, 16 + 8 * tile))] = value
        else:
            ref[(*index, slice(24, 28))] = value[0:4]
            ref[(*index, slice(4, 8))] = value[4:8]

    def from_slot(packed, slot):
        return pltpu.roll(packed, (124 - 8 * slot) % 128, 1)

    for up in range(2):
        for tile in range(3):
            both = merged(RZ[0, up, tile], RZ[1, up, tile])
            ok = side_ok * (high_z_ok if up else low_z_ok)
            ok = ok * halo_rows_ok if tile == 2 else ok
            slot = 0
            for f, deep in edge_slots:
                for p in range(deep):
                    at = 20 + p if up else 4 - deep + p
                    piece = from_slot(both, slot)
                    slot += 1
                    if f < 4:
                        spread(F, (f, 1, at), tile, piece)
                    else:
                        hr, hi = look_up(piece, (0, 1))
                        spread(H, (0, 1, at), tile, hr * ok)
                        spread(H, (1, 1, at), tile, hi * ok)
        for p in range(3):
            at = 20 + p if up else 1 + p
            ok = high_z_ok if up else low_z_ok
            for yg, y_ok in enumerate((low_y_ok, 1.0, 1.0, high_y_ok)):
                rows = slice(8 * yg, 8 * yg + 8)
                hr, hi = look_up(F[4, 0, at, rows], (0, 1))
                H[0, 0, at, rows] = hr * (ok * y_ok)
                H[1, 0, at, rows] = hi * (ok * y_ok)

    def halo_coefficients(z, carry):
        shift = 124 - 8 * (z - 4)
        for tile in range(3):
            hr, hi = look_up(pltpu.roll(merged(RL[0, tile], RL[1, tile]), shift, 1), (0, 1))
            ok = side_ok * halo_rows_ok if tile == 2 else side_ok
            spread(H, (0, 1, z), tile, hr * ok)
            spread(H, (1, 1, z), tile, hi * ok)
        for rows, ok in ((slice(0, 8), low_y_ok), (slice(24, 32), high_y_ok)):
            hr, hi = look_up(F[4, 0, z, rows], (0, 1))
            H[0, 0, z, rows] = hr * ok
            H[1, 0, z, rows] = hi * ok
        return carry

    lax.fori_loop(4, 20, halo_coefficients, 0, unroll=8)

    for copy in started[len(first_group) :]:
        copy.wait()
    loads[3].wait()

    def unpack_quarter(zq, carry):
        for tile in range(3):
            both = merged(RU[0, zq, tile], RU[1, zq, tile])
            for f in range(4):
                for p in range(4):
                    spread(F, (f, 1, 4 + 4 * zq + p), tile, from_slot(both, 4 * f + p))
        return carry

    lax.fori_loop(0, 4, unpack_quarter, 0, unroll=4)

    pl.semaphore_wait(ready.at[0], met)
    met = greet(ready.at[1], [(2, 0, 0), (-2, 0, 0), (0, 2, 0), (0, -2, 0)])

    @pl.when(gz == 0)
    def _():
        F[0:2, :, 0:4] = jnp.zeros((2, 2, 4, 32, 128), F32)
        G[:, 0, 1] = jnp.zeros((2, 32, 128), F32)

    @pl.when(gz == nz - 1)
    def _():
        F[0:2, :, 20:24] = jnp.zeros((2, 2, 4, 32, 128), F32)
        G[:, 0, 10] = jnp.zeros((2, 32, 128), F32)

    @pl.when(gy == 0)
    def _():
        F[0:2, :, :, 4:8] = jnp.zeros((2, 2, 24, 4, 128), F32)
        G[:, 0, :, 4:8] = jnp.zeros((2, 12, 4, 128), F32)

    @pl.when(gy == ny - 1)
    def _():
        F[0:2, :, :, 24:28] = jnp.zeros((2, 2, 24, 4, 128), F32)
        G[:, 0, :, 24:28] = jnp.zeros((2, 12, 4, 128), F32)

    for yh in range(2):
        both = merged(RG[0, yh], RG[1, yh])
        for c in range(2):
            for z in range(8):
                G[c, 1, 2 + z, 8 + 8 * yh : 16 + 8 * yh] = pltpu.roll(both, (124 - 8 * (8 * c + z)) % 128, 1)

    def across(main, ext, step, tiles):
        at = lax.broadcasted_iota(jnp.int32, main.shape, 1)
        low, high = at < step, at >= 128 - step
        ml, el = pltpu.roll(main, step, 1), pltpu.roll(ext, step, 1)
        mr, er = pltpu.roll(main, 128 - step, 1), pltpu.roll(ext, 128 - step, 1)
        out = [jnp.where(low, el, ml) + jnp.where(high, er, mr)]
        if tiles == 2:
            out.append(jnp.where(low, ml, el) + jnp.where(high, mr, er))
        return out

    def sweep(source, target, first, last):
        def plane(z, carry):
            for rows in (4, 12, 20):
                mid = pl.ds(rows, 8)
                near = [[None, None], [None, None]]
                centre = [[None, None], [None, None]]
                for c in range(2):
                    main, ext = source[c, 0, z, mid], source[c, 1, z, mid]
                    centre[c] = [main, ext]
                    side = across(main, ext, 1, 2)
                    for t in range(2):
                        near[c][t] = (
                            side[t]
                            + (source[c, t, z - 1, mid] + source[c, t, z + 1, mid])
                            + (source[c, t, z, pl.ds(rows - 1, 8)] + source[c, t, z, pl.ds(rows + 1, 8)])
                        )
                for t in range(2):
                    wr = F[2, t, z, mid] + near[0][t]
                    wi = F[3, t, z, mid] + near[1][t]
                    hr, hi = H[0, t, z, mid], H[1, t, z, mid]
                    target[0, t, z, mid] = 0.5 * centre[0][t] + (hr * wr - hi * wi)
                    target[1, t, z, mid] = 0.5 * centre[1][t] + (hr * wi + hi * wr)
            return carry

        lax.fori_loop(first, last, plane, 0, unroll=(last - first) // 2)

    sweep(F, B, 1, 23)
    sweep(B, F, 2, 22)
    sweep(F, B, 3, 21)

    pl.semaphore_wait(ready.at[1], met)
    met = greet(ready.at[2], [(0, 4, 0), (0, -4, 0)])

    zero = jnp.zeros((8, 128), F32)

    def residual(zc, carry):
        src_sq, pre_sq = carry
        for yh in range(2):
            rows = 8 + 8 * yh
            mid, out = pl.ds(rows, 8), slice(8 * yh, 8 * yh + 8)
            sums = [zero, zero]
            for k in range(2):
                z = 2 * zc + k
                near, centre = [], []
                for c in range(2):
                    main = B[c, 0, z + 4, mid]
                    centre.append(main)
                    side = across(main, B[c, 1, z + 4, mid], 1, 1)[0]
                    near.append(
                        side
                        + (B[c, 0, z + 3, mid] + B[c, 0, z + 5, mid])
                        + (B[c, 0, z + 4, pl.ds(rows - 1, 8)] + B[c, 0, z + 4, pl.ds(rows + 1, 8)])
                    )
                dr, di = D[0, z, out], D[1, z, out]
                sr, si = F[2, 0, z + 4, mid], F[3, 0, z + 4, mid]
                rr = sr + near[0] - (dr * centre[0] - di * centre[1])
                ri = si + near[1] - (dr * centre[1] + di * centre[0])
                RP[0, z, out] = rr
                RP[1, z, out] = ri
                src_sq = src_sq + (sr * sr + si * si)
                pre_sq = pre_sq + (rr * rr + ri * ri)
                sums = [sums[0] + rr, sums[1] + ri]
            br, bi = 0.5 * block_sum(sums[0]), 0.5 * block_sum(sums[1])
            wr, wi = G[0, 0, zc + 2, mid], G[1, 0, zc + 2, mid]
            E[0, 0, zc + 2, mid] = wr * br - wi * bi
            E[1, 0, zc + 2, mid] = wr * bi + wi * br
        return src_sq, pre_sq

    src_sq, pre_sq = lax.fori_loop(0, 8, residual, (zero, zero), unroll=8)

    del started[:]
    for offset in order:
        dx, dy, dz = offset
        if dx == 0:
            from_z, to_z = planes(dz, 8, 1 if dy else 2, 2)
            from_y, to_y = planes(dy, 16, 4, 8)
            send(offset, E.at[:, 0, from_z, from_y], E.at[:, 0, to_z, to_y], send_c, recv_c)
    for yh in range(2):
        PE[yh] = pack([E[c, 0, 2 + z, 8 + 8 * yh : 16 + 8 * yh] for c in range(2) for z in range(8)])
    for offset in order:
        dx, dy, dz = offset
        if dx and not (dy and dz):
            side = 0 if dx > 0 else 1
            from_y, to_y, rows = tiles(dy)
            send(offset, PE.at[from_y, rows], RE.at[side, 1 - dz, to_y, rows], send_c, recv_c)
    for copy in started:
        copy.wait()

    for part, where in ((1, range(8)), (0, (7,)), (2, (0,))):
        for tile in range(3 if part == 1 else 2):
            both = merged(RE[0, part, tile], RE[1, part, tile])
            for c in range(2):
                for z in where:
                    at = 2 + z if part == 1 else (1 if part == 0 else 10)
                    spread(E, (c, 1, at), tile, from_slot(both, 8 * c + z))

    @pl.when(gz == 0)
    def _():
        E[:, :, 0:2] = jnp.zeros((2, 2, 2, 32, 128), F32)

    @pl.when(gz == nz - 1)
    def _():
        E[:, :, 10:12] = jnp.zeros((2, 2, 2, 32, 128), F32)

    @pl.when(gy == 0)
    def _():
        E[:, :, :, 4:8] = jnp.zeros((2, 2, 12, 4, 128), F32)

    @pl.when(gy == ny - 1)
    def _():
        E[:, :, :, 24:28] = jnp.zeros((2, 2, 12, 4, 128), F32)

    def coarse(zc, row_groups, tiles):
        for rows in row_groups:
            mid = pl.ds(rows, 8)
            near, centre = [], []
            for c in range(2):
                main, ext = E[c, 0, zc, mid], E[c, 1, zc, mid]
                side = across(main, ext, 2, tiles)
                centre.append([main, ext])
                near.append(
                    [
                        side[t]
                        + (E[c, t, zc - 1, mid] + E[c, t, zc + 1, mid])
                        + (E[c, t, zc, pl.ds(rows - 2, 8)] + E[c, t, zc, pl.ds(rows + 2, 8)])
                        for t in range(tiles)
                    ]
                )
            for t in range(tiles):
                wr, wi = G[0, t, zc, mid], G[1, t, zc, mid]
                E1[0, t, zc, mid] = 1.5 * centre[0][t] + (wr * near[0][t] - wi * near[1][t])
                E1[1, t, zc, mid] = 1.5 * centre[1][t] + (wr * near[1][t] + wi * near[0][t])

    def own_planes(zc, carry):
        coarse(zc, (8, 16), 2)
        coarse(zc, (4, 20), 1)
        return carry

    lax.fori_loop(2, 10, own_planes, 0, unroll=8)
    coarse(1, (8, 16), 1)
    coarse(10, (8, 16), 1)

    def correct(zc, carry):
        carry = list(carry)
        for yh in range(2):
            rows = 8 + 8 * yh
            mid, out = pl.ds(rows, 8), slice(8 * yh, 8 * yh + 8)
            e, base = [], []
            for c in range(2):
                main = E1[c, 0, zc + 2, mid]
                side = across(main, E1[c, 1, zc + 2, mid], 1, 1)[0]
                e.append(main)
                base.append(
                    main + side + (E1[c, 0, zc + 2, pl.ds(rows - 1, 8)] + E1[c, 0, zc + 2, pl.ds(rows + 1, 8)])
                )
            for k in range(2):
                z = 2 * zc + k
                dr, di = D[0, z, out], D[1, z, out]
                rr = RP[0, z, out] + (base[0] + E1[0, 0, zc + 1 + 2 * k, mid]) - (dr * e[0] - di * e[1])
                ri = RP[1, z, out] + (base[1] + E1[1, 0, zc + 1 + 2 * k, mid]) - (dr * e[1] + di * e[0])
                carry[0] = carry[0] + (rr * rr + ri * ri)
                ar = B[0, 0, z + 4, mid] + e[0]
                ai = B[1, 0, z + 4, mid] + e[1]
                ADJ[0, z, out] = ar
                ADJ[1, z, out] = ai
                fr, fi = FW[0, z, out], FW[1, z, out]
                pr = fr * ar - fi * ai
                pi = fr * ai + fi * ar
                label = LI[z, out]
                for m in range(NMAT):
                    chosen = label == m
                    carry[1 + m] = carry[1 + m] + jnp.where(chosen, pr, 0.0)
                    carry[9 + m] = carry[9 + m] + jnp.where(chosen, pi, 0.0)
        return tuple(carry)

    sums = lax.fori_loop(0, 8, correct, (zero,) * 17, unroll=2)
    store = pltpu.make_async_copy(ADJ, adj_hbm, local_sem.at[0])
    store.start()

    pl.semaphore_wait(ready.at[2], met)

    ordered = list(sums[1:]) + [src_sq, pre_sq, sums[0]]
    ACC[...] = jnp.zeros((24, 128), F32)
    for k, value in enumerate(ordered):
        ACC[k : k + 1] = jnp.sum(value, axis=0, keepdims=True)
    totals = jnp.sum(ACC[...], axis=1, keepdims=True)
    lane24 = lax.broadcasted_iota(jnp.int32, (24, 128), 1)
    row24 = lax.broadcasted_iota(jnp.int32, (24, 128), 0)
    row = jnp.sum(jnp.where(lane24 == row24, totals, 0.0), axis=0, keepdims=True)

    for stage, (peers, slots, own) in enumerate(((y_peers, R1, gy), (xz_peers, R2, gx * nz + gz))):
        count = len(peers)
        VAL[stage] = row
        for offset in peers:
            pltpu.make_async_remote_copy(
                src_ref=VAL.at[stage],
                dst_ref=slots.at[own],
                send_sem=send_r.at[stage],
                recv_sem=recv_r.at[stage],
                device_id=device(offset),
                device_id_type=MESH,
            ).start()
        slots[own] = row
        every = pltpu.make_async_remote_copy(
            src_ref=slots.at[pl.ds(0, count)],
            dst_ref=slots.at[pl.ds(0, count)],
            send_sem=send_r.at[stage],
            recv_sem=recv_r.at[stage],
            device_id=device(peers[0]),
            device_id_type=MESH,
        )
        every.wait_recv()
        every.wait_send()
        row = slots[0]
        for k in range(1, count + 1):
            row = row + slots[k]

    cells = float(nx * ny * nz * 16 * 16 * 128)
    one = lax.broadcasted_iota(jnp.int32, (1, 128), 1)
    row_ref[...] = jnp.where(one < 2 * NMAT, (-KH2 / cells**0.5) * row, jnp.sqrt(jnp.maximum(row, 0.0) / cells))
    store.wait()


def finish(adjoint, row_ref, out, grad, norms):
    out[...] = adjoint[...]
    row = row_ref[...]
    grad[0:1] = row[:, :NMAT]
    grad[1:2] = pltpu.roll(row, 128 - NMAT, 1)[:, :NMAT]
    norms[...] = pltpu.roll(row, 128 - 2 * NMAT, 1)[0, :3]


def shards(sizes, source, adjoint_guess, forward_field, labels, perm_real, perm_imag):
    vmem = lambda *shape: pltpu.VMEM(shape, F32)
    dma = pltpu.SemaphoreType.DMA
    n_a, n_c = 54, 18
    adjoint, row = pl.pallas_call(
        functools.partial(kernel, sizes),
        out_shape=(
            jax.ShapeDtypeStruct(adjoint_guess.shape, F32),
            jax.ShapeDtypeStruct((1, 128), F32),
        ),
        in_specs=[pl.BlockSpec(memory_space=pltpu.HBM)] * 4 + [pl.BlockSpec(memory_space=pltpu.SMEM)] * 2,
        out_specs=(pl.BlockSpec(memory_space=pltpu.HBM), pl.BlockSpec(memory_space=pltpu.VMEM)),
        scratch_shapes=[
            vmem(5, 2, 24, 32, 128),
            vmem(2, 2, 24, 32, 128),
            vmem(2, 2, 24, 32, 128),
            vmem(2, 16, 16, 128),
            vmem(2, 16, 16, 128),
            pltpu.VMEM((16, 16, 128), jnp.int32),
            vmem(2, 16, 16, 128),
            vmem(2, 2, 12, 32, 128),
            vmem(2, 2, 12, 32, 128),
            vmem(2, 2, 12, 32, 128),
            vmem(2, 16, 16, 128),
            vmem(16, 16, 128),
            vmem(5, 8, 8, 128),
            vmem(4, 2, 8, 128),
            vmem(2, 8, 128),
            vmem(2, 8, 128),
            vmem(2, 8, 128),
            vmem(2, 2, 8, 128),
            vmem(2, 4, 3, 8, 128),
            vmem(2, 3, 8, 128),
            vmem(2, 2, 3, 8, 128),
            vmem(2, 2, 8, 128),
            vmem(2, 3, 3, 8, 128),
            vmem(24, 128),
            vmem(2, 1, 128),
            vmem(sizes[1], 1, 128),
            vmem(sizes[0] * sizes[2], 1, 128),
            dma((4,)),
            dma((n_a,)),
            dma((n_a,)),
            dma((n_c,)),
            dma((n_c,)),
            dma((2,)),
            dma((2,)),
            pltpu.SemaphoreType.REGULAR((3,)),
        ],
        compiler_params=pltpu.CompilerParams(collective_id=0, has_side_effects=True, vmem_limit_bytes=20 << 20),
    )(*(pltpu.with_memory_space_constraint(a, pltpu.HBM) for a in (adjoint_guess, source, forward_field, labels, perm_real, perm_imag)))
    return pl.pallas_call(
        finish,
        out_shape=(
            jax.ShapeDtypeStruct(adjoint_guess.shape, F32),
            jax.ShapeDtypeStruct((2, NMAT), F32),
            jax.ShapeDtypeStruct((3,), F32),
        ),
        in_specs=[pl.BlockSpec(memory_space=pltpu.VMEM)] * 2,
        out_specs=(pl.BlockSpec(memory_space=pltpu.VMEM),) * 3,
    )(*(pltpu.with_memory_space_constraint(a, pltpu.VMEM) for a in (adjoint, row)))


def solution(mesh):
    sizes = tuple(mesh.shape[a] for a in AXES)
    field = P(None, "gz", "gy", "gx")
    return jax.shard_map(
        functools.partial(shards, sizes),
        mesh=mesh,
        in_specs=(field, field, field, P("gz", "gy", "gx"), P(), P()),
        out_specs=(field, P(), P()),
        check_vma=False,
    )
```
